128 devices in a mesh: dp: 16 (over y, z), seq: 8 (over x, core).
Axes of the slice: x: 4, y: 4, z: 4, core: 2. Of those that a mesh axis runs over, the one named last changes fastest.
Arguments:
- inputs: bfloat16 [16, 1024, 768], P('dp', 'seq'), may hold values from -6 to 6
- encoded: bfloat16 [16, 256, 768], P('dp', 'seq'), may hold values from -6 to 6
- cotangent: bfloat16 [16, 1024, 768], P('dp', 'seq'), may hold values from -6 to 6
- buckets: int32 [1024], replicated, may hold values from 0 to 31
- bias_table: bfloat16 [32, 12], replicated, may hold values from -4 to 4
- norm_self: bfloat16 [768], P(('dp', 'seq')), may hold values from 0.5 to 1.5
- norm_cross: bfloat16 [768], P(('dp', 'seq')), may hold values from 0.5 to 1.5
- norm_feed: bfloat16 [768], P(('dp', 'seq')), may hold values from 0.5 to 1.5
- self_query: bfloat16 [768, 768], P(('dp', 'seq')), may hold values from -0.0546875 to 0.0546875
- self_key: bfloat16 [768, 768], P(('dp', 'seq')), may hold values from -0.21875 to 0.21875
- self_value: bfloat16 [768, 768], P(('dp', 'seq')), may hold values from -0.21875 to 0.21875
- self_out: bfloat16 [768, 768], P(('dp', 'seq')), may hold values from -0.875 to 0.875
- cross_query: bfloat16 [768, 768], P(('dp', 'seq')), may hold values from -0.0546875 to 0.0546875
- cross_key: bfloat16 [768, 768], P(('dp', 'seq')), may hold values from -0.21875 to 0.21875
- cross_value: bfloat16 [768, 768], P(('dp', 'seq')), may hold values from -0.21875 to 0.21875
- cross_out: bfloat16 [768, 768], P(('dp', 'seq')), may hold values from -0.875 to 0.875
- feed_gate: bfloat16 [768, 2048], P(('dp', 'seq')), may hold values from -0.21875 to 0.21875
- feed_up: bfloat16 [768, 2048], P(('dp', 'seq')), may hold values from -0.21875 to 0.21875
- feed_down: bfloat16 [2048, 768], P(('dp', 'seq')), may hold values from -0.125 to 0.125
Outputs:
- output: bfloat16 [16, 1024, 768], P('dp', 'seq')
- grad_inputs: float32 [16, 1024, 768], P('dp', 'seq')
- grad_encoded: float32 [16, 256, 768], P('dp', 'seq')
- grad_table: float32 [32, 12], replicated
- grad_norm_self: float32 [768], P(('dp', 'seq'))
- grad_norm_cross: float32 [768], P(('dp', 'seq'))
- grad_norm_feed: float32 [768], P(('dp', 'seq'))
- grad_self_query: float32 [768, 768], P(('dp', 'seq'))
- grad_self_key: float32 [768, 768], P(('dp', 'seq'))
- grad_self_value: float32 [768, 768], P(('dp', 'seq'))
- grad_self_out: float32 [768, 768], P(('dp', 'seq'))
- grad_cross_query: float32 [768, 768], P(('dp', 'seq'))
- grad_cross_key: float32 [768, 768], P(('dp', 'seq'))
- grad_cross_value: float32 [768, 768], P(('dp', 'seq'))
- grad_cross_out: float32 [768, 768], P(('dp', 'seq'))
- grad_feed_gate: float32 [768, 2048], P(('dp', 'seq'))
- grad_feed_up: float32 [768, 2048], P(('dp', 'seq'))
- grad_feed_down: float32 [2048, 768], P(('dp', 'seq'))
The draws below stay inside these ranges and needn't reach their ends.
All inputs are finite; a program needn't handle non-finite values.
Results may differ from the reference program's by a relative error of at most 0.04.
Values may be sent and summed in bfloat16 or wider, within the bound.
No kernel may reach another device: no remote copies, remote signals or barrier semaphores. Data moves between devices by JAX's collectives and lax.ppermute only.
A program may use at most 256 MiB of HBM per device.

```python
import jax
import jax.numpy as jnp
from jax import lax

D = 768
HEADS = 12
HEAD_DIM = 64
FF = 2048
BUCKETS = 32
LEN = 1024
ENC = 256
SEQS = 16


def touch_ends(values, stream_key, smallest, high):
    longest = values.shape.index(max(values.shape))
    spots = []
    for shift in (0, 1):
        where = [jax.random.randint(jax.random.fold_in(stream_key, axis), (), 0, length) for axis, length in enumerate(values.shape)]
        where[longest] = (where[longest] + shift) % values.shape[longest]
        spots.append(tuple(where))
    return values.at[spots[0]].set(smallest).at[spots[1]].set(high)


def steps_of(rng, shape, pieces, least, high):
    level, own = 1.0, jax.random.fold_in(rng, 6)
    for dim, blocks in pieces:
        heights = jnp.exp(jax.random.uniform(jax.random.fold_in(own, dim), (blocks,), jnp.float32, least / len(pieces), high / len(pieces)))
        level = level * jnp.repeat(heights, shape[dim] // blocks).reshape([-1 if axis == dim else 1 for axis in range(len(shape))])
    return level


def normal_values(key, dims, deviation, reach, pieces=(), held_as=jnp.bfloat16):
    values = jax.random.normal(key, dims, jnp.float32) * deviation
    if len(pieces) > 0:
        values = steps_of(key, dims, pieces, -0.22, 0.18) * values
    return jnp.clip(values, min=-reach, max=reach).astype(held_as)


def setup_inputs(seed: int = 0) -> dict:
    splits = jax.random.split(jax.random.key(seed), 20)
    inputs = normal_values(splits[0], (SEQS, LEN, D), 1.0, 6.0, ((0, 16), (1, 8)))
    encoded = normal_values(splits[1], (SEQS, ENC, D), 1.0, 6.0, ((0, 16), (1, 8)))
    cotangent = normal_values(splits[2], (SEQS, LEN, D), 1.0, 6.0, ((0, 16), (1, 8)))
    buckets = touch_ends(jax.random.randint(splits[3], (LEN,), 0, BUCKETS), jax.random.fold_in(splits[3], 1), 0, BUCKETS - 1).astype(jnp.int32)
    bias_table = normal_values(splits[4], (BUCKETS, HEADS), 1.0, 4.0)
    norm_self = jnp.clip(1.0 + 0.1 * jax.random.normal(splits[5], (D,), jnp.float32), 0.5, 1.5).astype(jnp.bfloat16)
    norm_cross = jnp.clip(1.0 + 0.1 * jax.random.normal(splits[6], (D,), jnp.float32), 0.5, 1.5).astype(jnp.bfloat16)
    norm_feed = jnp.clip(1.0 + 0.1 * jax.random.normal(splits[7], (D,), jnp.float32), 0.5, 1.5).astype(jnp.bfloat16)
    self_query = normal_values(splits[8], (D, D), (16 * D) ** -0.5, 0.0546875, ((0, 128),))
    self_key = normal_values(splits[9], (D, D), D ** -0.5, 0.21875, ((0, 128),))
    self_value = normal_values(splits[10], (D, D), D ** -0.5, 0.21875, ((0, 128),))
    self_out = normal_values(splits[11], (D, D), (D // 16) ** -0.5, 0.875, ((0, 128),))
    cross_query = normal_values(splits[12], (D, D), (16 * D) ** -0.5, 0.0546875, ((0, 128),))
    cross_key = normal_values(splits[13], (D, D), D ** -0.5, 0.21875, ((0, 128),))
    cross_value = normal_values(splits[14], (D, D), D ** -0.5, 0.21875, ((0, 128),))
    cross_out = normal_values(splits[15], (D, D), (D // 16) ** -0.5, 0.875, ((0, 128),))
    feed_gate = normal_values(splits[16], (D, FF), D ** -0.5, 0.21875, ((0, 128),))
    feed_up = normal_values(splits[17], (D, FF), D ** -0.5, 0.21875, ((0, 128),))
    feed_down = normal_values(splits[18], (FF, D), FF ** -0.5, 0.125, ((0, 128),))
    return {"inputs": inputs, "encoded": encoded, "cotangent": cotangent, "buckets": buckets, "bias_table": bias_table, "norm_self": norm_self, "norm_cross": norm_cross, "norm_feed": norm_feed, "self_query": self_query, "self_key": self_key, "self_value": self_value, "self_out": self_out, "cross_query": cross_query, "cross_key": cross_key, "cross_value": cross_value, "cross_out": cross_out, "feed_gate": feed_gate, "feed_up": feed_up, "feed_down": feed_down}


@jax.custom_vjp
def low(v):
    return lax.optimization_barrier(v.astype(jnp.bfloat16)).astype(jnp.float32)

@jax.custom_vjp
def low_back(v):
    return v

def low_keep(v):
    return (low(v), None)

def low_pass(kept, grad):
    return (grad,)

def back_keep(v):
    return (v, None)

def back_low(kept, grad):
    return (low(grad),)
low.defvjp(low_keep, low_pass)
low_back.defvjp(back_keep, back_low)
epsilon = 1e-06
masked = -1e+30

def both(values):
    return low(low_back(values))

def product(left, right):
    return jnp.dot(left, right, precision=lax.Precision.HIGHEST)

def rms_scale(values, gain):
    return values * lax.rsqrt(lax.optimization_barrier(jnp.mean(values * values, axis=-1, keepdims=True)) + epsilon) * gain

def gelu_tanh(values):
    return 0.5 * values * (1.0 + jnp.tanh(0.7978845608028654 * (values + 0.044715 * values * values * values)))

def attend(query, keys, values, bias, allowed):
    count = query.shape[0]
    query_heads = query.reshape(count, HEADS, HEAD_DIM)
    key_heads = keys.reshape(keys.shape[0], HEADS, HEAD_DIM)
    value_heads = values.reshape(values.shape[0], HEADS, HEAD_DIM)
    raw = low_back(jnp.einsum('qhd,khd->hqk', query_heads, key_heads, precision=lax.Precision.HIGHEST))
    scores = jnp.where(allowed, raw + bias, masked)
    shares = jax.nn.softmax(scores, axis=-1)
    mixed = jnp.einsum('hqk,khd->qhd', low(shares), value_heads, precision=lax.Precision.HIGHEST)
    return both(mixed.reshape(count, HEADS * HEAD_DIM))

def layer(params, table, resid, states, buckets):
    norm_self, norm_cross, norm_feed, self_query, self_key, self_value, self_out, cross_query, cross_key, cross_value, cross_out, feed_gate, feed_up, feed_down = params
    low_one = low(rms_scale(resid, norm_self))
    query = both(product(low_one, self_query))
    keys = both(product(low_one, self_key))
    values = both(product(low_one, self_value))
    places = jnp.arange(LEN)
    offset = places[:, None] - places[None, :]
    bias = jnp.transpose(table[buckets[jnp.clip(offset, 0, LEN - 1)]], (2, 0, 1))
    mixed = attend(query, keys, values, bias, offset >= 0)
    after_self = resid + low_back(product(mixed, self_out))
    low_two = low(rms_scale(after_self, norm_cross))
    query_two = both(product(low_two, cross_query))
    keys_two = both(product(states, cross_key))
    values_two = both(product(states, cross_value))
    mixed_two = attend(query_two, keys_two, values_two, 0.0, True)
    after_cross = after_self + low_back(product(mixed_two, cross_out))
    low_three = low(rms_scale(after_cross, norm_feed))
    gate = low_back(product(low_three, feed_gate))
    upper = low_back(product(low_three, feed_up))
    hidden = low(gelu_tanh(gate) * upper)
    return after_cross + low_back(product(hidden, feed_down))

def reference(inputs, encoded, cotangent, buckets, bias_table, norm_self, norm_cross, norm_feed, self_query, self_key, self_value, self_out, cross_query, cross_key, cross_value, cross_out, feed_gate, feed_up, feed_down):
    params = tuple((item.astype(jnp.float32) for item in (norm_self, norm_cross, norm_feed, self_query, self_key, self_value, self_out, cross_query, cross_key, cross_value, cross_out, feed_gate, feed_up, feed_down)))
    table = bias_table.astype(jnp.float32)

    def forward(weights, table_in, resid, states):

        def one_sequence(pair):
            return layer(weights, table_in, pair[0], pair[1], buckets)
        return lax.map(jax.checkpoint(one_sequence), (resid, states))
    result, pull = jax.vjp(forward, params, table, inputs.astype(jnp.float32), encoded.astype(jnp.float32))
    grad_params, grad_table, grad_inputs, grad_encoded = pull(cotangent.astype(jnp.float32))
    return (result.astype(jnp.bfloat16), grad_inputs, grad_encoded, grad_table, grad_params[0], grad_params[1], grad_params[2], grad_params[3], grad_params[4], grad_params[5], grad_params[6], grad_params[7], grad_params[8], grad_params[9], grad_params[10], grad_params[11], grad_params[12], grad_params[13])
```

```python
import functools

import jax
import jax.numpy as jnp
from jax import lax
from jax.experimental import pallas as pl
from jax.experimental.pallas import tpu as pltpu
from jax.sharding import Mesh
from jax.sharding import PartitionSpec as P

HEADS = 12
PAIRS = HEADS // 2
EPS = 1e-06
MASKED = -1e30
BF = jnp.bfloat16
F32 = jnp.float32
ALL = ("y", "z", "x", "c")
CHIPS = ("y", "z", "x")
ROWS = ("y", "z")
SEQ = ("x", "c")
SWAP = [(0, 1), (1, 0)]
PARAMS = pltpu.CompilerParams(vmem_limit_bytes=56 * 1024 * 1024)


def other_core(a):
    return lax.ppermute(a, "c", SWAP)


def exchange(a, axes):
    return lax.all_to_all(a, axes, 0, 0, tiled=True)


def copies(a, axes, count):
    return exchange(jnp.broadcast_to(a[None], (count, *a.shape)), axes)


def shifted(a, by):
    return lax.ppermute(a, "x", [((i + by) % 4, i) for i in range(4)])


def around_x(a):
    own = jnp.concatenate([a, *(shifted(a, by) for by in (1, 2, 3))], axis=0)
    return own, other_core(own)


def gathered(a, axis):
    place = lax.axis_index(axis)
    whole = jnp.zeros((4, *a.shape), a.dtype)
    for by in range(4):
        part = a
        if by:
            part = lax.ppermute(a, axis, [((i + by) % 4, i) for i in range(4)])
        whole = lax.dynamic_update_index_in_dim(whole, part, lax.rem(place + by, 4), 0)
    return whole


def back_around_x(parts):
    rows = parts.shape[0] // 4
    own, *others = [parts[rows * n : rows * n + rows] for n in range(4)]
    return own.astype(F32) + sum(shifted(a, -by).astype(F32) for by, a in enumerate(others, 1))


def to_owner(own, other):
    both = (own.astype(F32) + other_core(other).astype(F32)).astype(BF)
    return back_around_x(both)


def after(a, *earlier):
    return lax.optimization_barrier((a, *earlier))[0]


def cost(us):
    return pl.CostEstimate(flops=int(us * 1.0e9), bytes_accessed=int(us * 1.0e6), transcendentals=0)


def dot(a, b):
    return jnp.dot(a, b, preferred_element_type=F32)


def dot_t(a, b):
    return lax.dot_general(a, b, (((1,), (1,)), ((), ())), preferred_element_type=F32)


def t_dot(a, b):
    return lax.dot_general(a, b, (((0,), (0,)), ((), ())), preferred_element_type=F32)


def normed(v):
    r = lax.rsqrt(jnp.mean(v * v, axis=-1, keepdims=True) + EPS)
    return v * r, r


def norm_back(g, hat, r, gain):
    scaled = g * gain
    return r * (scaled - hat * jnp.mean(scaled * hat, axis=-1, keepdims=True))


def gelu(v):
    return 0.5 * v * (1.0 + jnp.tanh(0.7978845608028654 * (v + 0.044715 * v * v * v)))


def gather_rows_kernel(count, *refs):
    weights, out, rows = refs[:count], refs[-2], refs[-1]
    for m, w in enumerate(weights):
        rows[6 * m : 6 * m + 6] = w[...].astype(F32)
    if len(refs) == count + 3:
        row = lax.broadcasted_iota(jnp.int32, (8, 128), 0)
        lane = lax.broadcasted_iota(jnp.int32, (8, 128), 1)
        unit = (row == lane).astype(F32)
        wide = jnp.concatenate([refs[count][...], jnp.zeros((120, 128), F32)], axis=0)
        rows[6 * count :] = jnp.zeros((8, 768), F32)
        rows[6 * count :, :128] = dot_t(unit, wide)
    out[...] = rows[...].astype(BF)


def packed_rows(weights, norms=()):
    count = len(weights)
    total = 6 * count + (8 if norms else 0)
    more = [jnp.pad(jnp.stack(norms).astype(F32), ((0, 5), (0, 122)))] if norms else []
    return pl.pallas_call(
        functools.partial(gather_rows_kernel, count),
        out_shape=jax.ShapeDtypeStruct((total, 768), BF),
        scratch_shapes=[pltpu.VMEM((total, 768), F32)],
        compiler_params=PARAMS,
        cost_estimate=cost(2),
        name="packed_rows",
    )(*weights, *more)


def unpack_kernel(ways, place_ref, *refs):
    packed, outs = refs[:ways], refs[ways:]
    step = packed[0].shape[0] // 4 * ways
    for b in range(4):
        if ways == 1:
            rows = packed[0][step * b : step * b + step]
        else:
            rows = jnp.concatenate(
                [p[step // 2 * b : step // 2 * b + step // 2] for p in packed], axis=0
            )
        half = rows.shape[0] // 2
        halves = [dot(place_ref[...], rows[half * n : half * n + half]) for n in range(2)] if (
            ways == 1
        ) else [dot(place_ref[...], rows)]
        for m, out in enumerate(outs):
            size = 24 if ways == 1 else 48
            piece = jnp.concatenate([h[size * m : size * m + size] for h in halves], axis=0)
            out[48 * b : 48 * b + 48] = piece[:, : out.shape[1]].astype(BF)


def unpack_four(packed):
    q = jnp.arange(96, dtype=jnp.int32)
    source = (q % 24) // 6 * 24 + q // 24 * 6 + q % 6
    place = (source[:, None] == jnp.arange(96, dtype=jnp.int32)[None, :]).astype(BF)
    return pl.pallas_call(
        functools.partial(unpack_kernel, 1),
        grid=(4,),
        in_specs=[
            pl.BlockSpec((96, 96), lambda b: (0, 0)),
            pl.BlockSpec((768, 768), lambda b: (b, 0)),
        ],
        out_specs=[pl.BlockSpec((192, 768), lambda b: (b, 0))] * 4,
        out_shape=[jax.ShapeDtypeStruct((768, 768), BF)] * 4,
        compiler_params=PARAMS,
        cost_estimate=cost(5),
        name="unpack_four",
    )(place, packed)


def unpack_cores(core, mine, theirs):
    q = jnp.arange(240, dtype=jnp.int32)
    device, row = (q % 48) // 6, q // 48 * 6 + q % 6
    source = (device % 2 ^ core) * 128 + device // 2 * 32 + row
    place = (source[:, None] == jnp.arange(256, dtype=jnp.int32)[None, :]).astype(BF)
    return pl.pallas_call(
        functools.partial(unpack_kernel, 2),
        grid=(4,),
        in_specs=[
            pl.BlockSpec((240, 256), lambda b: (0, 0)),
            pl.BlockSpec((512, 768), lambda b: (b, 0)),
            pl.BlockSpec((512, 768), lambda b: (b, 0)),
        ],
        out_specs=[pl.BlockSpec((192, 768), lambda b: (b, 0))] * 4
        + [pl.BlockSpec((192, 128), lambda b: (b, 0))],
        out_shape=[jax.ShapeDtypeStruct((768, 768), BF)] * 4
        + [jax.ShapeDtypeStruct((768, 128), BF)],
        compiler_params=PARAMS,
        cost_estimate=cost(6),
        name="unpack_cores",
    )(place, mine, theirs)


def pack_kernel(place_ref, a_ref, b_ref, c_ref, d_ref, *rest):
    out_ref = rest[-1]
    for b in range(4):
        rows = slice(48 * b, 48 * b + 48)
        four = jnp.concatenate([a_ref[rows], b_ref[rows], c_ref[rows], d_ref[rows]], axis=0)
        out_ref[192 * b : 192 * b + 192, :768] = dot(place_ref[...], four).astype(BF)
    if len(rest) == 2:
        out_ref[:, 768:] = rest[0][...]


def pack(four, extra=None):
    p = jnp.arange(192, dtype=jnp.int32)
    source = (p % 24) // 6 * 48 + p // 24 * 6 + p % 6
    place = (source[:, None] == p[None, :]).astype(BF)
    width = 768 if extra is None else 896
    more = [] if extra is None else [extra.reshape(1536, 128)]
    return pl.pallas_call(
        pack_kernel,
        grid=(2,),
        in_specs=[pl.BlockSpec((192, 192), lambda b: (0, 0))]
        + [pl.BlockSpec((192, 768), lambda b: (b, 0))] * 4
        + [pl.BlockSpec((768, 128), lambda b: (b, 0))] * len(more),
        out_specs=pl.BlockSpec((768, width), lambda b: (b, 0)),
        out_shape=jax.ShapeDtypeStruct((1536, width), BF),
        compiler_params=PARAMS,
        cost_estimate=cost(3.5),
        name="pack",
    )(place, *four, *more).reshape(64, 24, width)


def bias_kernel(line_ref, out_ref):
    for k in range(8):
        segment = line_ref[0, :, 128 * (7 - k) : 128 * (7 - k) + 256]
        wide = jnp.broadcast_to(segment, (128, 256))
        tile = pltpu.roll(wide, 129, 1, stride=1, stride_axis=0)
        out_ref[0, k] = tile[:, :128].astype(BF)


def bias_tiles(line):
    return pl.pallas_call(
        bias_kernel,
        grid=(HEADS,),
        in_specs=[pl.BlockSpec((1, 1, 1152), lambda h: (h, 0, 0))],
        out_specs=pl.BlockSpec((1, 8, 128, 128), lambda h: (h, 0, 0, 0)),
        out_shape=jax.ShapeDtypeStruct((HEADS, 8, 128, 128), BF),
        compiler_params=PARAMS,
        cost_estimate=cost(7.5),
        name="bias_tiles",
    )(line)


def half_lanes(shape, half):
    lane = lax.broadcasted_iota(jnp.int32, shape, 1)
    return (lane >= 64) if half else (lane < 64)


def block_offsets(place_ref):
    s, c, x = place_ref[0], place_ref[1], place_ref[2]
    return [
        s - (2 * lax.rem(x + n, 4) + (c if e == 0 else 1 - c)) for e in range(2) for n in range(4)
    ]


def add_bias(raw, bias_ref, half, away):
    i = lax.broadcasted_iota(jnp.int32, (128, 128), 0)
    j = lax.broadcasted_iota(jnp.int32, (128, 128), 1)
    parts = []
    for n, k in enumerate(away):
        tile = bias_ref[half, jnp.clip(k, 0, 7)].astype(F32)
        parts.append(
            jnp.where(i - j + 128 * k >= 0, raw[:, 128 * n : 128 * n + 128] + tile, MASKED)
        )
    return jnp.concatenate(parts, axis=1)


def forward_kernel(causal, pairs, place_ref, q_ref, k_ref, v_ref, *rest):
    bias_ref, out_ref = rest if causal else (None, rest[0])
    away = block_offsets(place_ref) if causal else None
    for pair in range(pairs):
        lanes = slice(128 * pair, 128 * pair + 128)
        keys, values, query = k_ref[:, lanes], v_ref[:, lanes], q_ref[:, lanes]
        mixed = []
        for half in range(2):
            low = half_lanes(query.shape, half)
            scores = dot_t(jnp.where(low, query, jnp.zeros_like(query)), keys)
            if causal:
                scores = add_bias(scores, bias_ref, 2 * pair + half, away)
            parts = jnp.exp(scores - jnp.max(scores, axis=-1, keepdims=True))
            share = 1.0 / jnp.sum(parts, axis=-1, keepdims=True)
            mixed.append(dot(parts.astype(BF), values) * share)
        out_ref[:, lanes] = jnp.where(half_lanes(mixed[0].shape, 0), mixed[0], mixed[1]).astype(BF)


def attend(place, query, keys, values, bias=None):
    causal = bias is not None
    rows, length = query.shape[0], keys.shape[0]
    pairs = 2 if causal else 6
    wide = 128 * pairs
    in_specs = [
        pl.BlockSpec(memory_space=pltpu.SMEM),
        pl.BlockSpec((rows, wide), lambda p: (0, p)),
        pl.BlockSpec((length, wide), lambda p: (0, p)),
        pl.BlockSpec((length, wide), lambda p: (0, p)),
    ]
    if causal:
        in_specs.append(pl.BlockSpec((2 * pairs, 8, 128, 128), lambda p: (p, 0, 0, 0)))
    return pl.pallas_call(
        functools.partial(forward_kernel, causal, pairs),
        grid=(PAIRS // pairs,),
        in_specs=in_specs,
        out_specs=pl.BlockSpec((rows, wide), lambda p: (0, p)),
        out_shape=jax.ShapeDtypeStruct((rows, 768), BF),
        compiler_params=PARAMS,
        cost_estimate=cost(7.5 if causal else 3),
        name="self_forward" if causal else "cross_forward",
    )(place, query, keys, values, *((bias,) if causal else ()))


def diagonal_sums(t):
    rows, width = t.shape
    while rows > 8:
        rows //= 2
        t = t[:rows] + pltpu.roll(t[rows:], width - rows, 1)
    row = lax.broadcasted_iota(jnp.int32, t.shape, 0)
    for step in (4, 2, 1):
        t = jnp.where((row & step) != 0, pltpu.roll(t, width - step, 1), t)
    return jnp.sum(t, axis=0, keepdims=True)


def backward_kernel(causal, pairs, place_ref, q_ref, k_ref, v_ref, g_ref, *rest):
    rows, length = q_ref.shape[0], k_ref.shape[0]
    if causal:
        bias_ref, out_ref, sums_ref, line_ref = rest
        away = block_offsets(place_ref)
        line_ref[:, :, length:] = jnp.zeros((2 * pairs, rows, 128), F32)
    else:
        (out_ref,) = rest
    for pair in range(pairs):
        lanes = slice(128 * pair, 128 * pair + 128)
        keys, values, query, grads = k_ref[:, lanes], v_ref[:, lanes], q_ref[:, lanes], g_ref[:, lanes]
        dq, dk, dv = [], 0.0, 0.0
        for half in range(2):
            low = half_lanes(query.shape, half)
            own_query = jnp.where(low, query, jnp.zeros_like(query))
            own_grads = jnp.where(low, grads, jnp.zeros_like(grads))
            scores = dot_t(own_query, keys)
            if causal:
                scores = add_bias(scores, bias_ref, 2 * pair + half, away)
            parts = jnp.exp(scores - jnp.max(scores, axis=-1, keepdims=True))
            shares = parts * (1.0 / jnp.sum(parts, axis=-1, keepdims=True))
            pushed = dot_t(own_grads, values)
            center = jnp.sum(shares * pushed, axis=-1, keepdims=True)
            ds = shares * (pushed - center)
            low_ds = ds.astype(BF)
            dq.append(dot(low_ds, keys))
            dk = dk + t_dot(low_ds, own_query)
            dv = dv + t_dot(shares.astype(BF), own_grads)
            if causal:
                for n, k in enumerate(away):
                    at = pl.multiple_of((place_ref[0] - k) * 128, 128)
                    line_ref[2 * pair + half, :, pl.ds(at, 128)] = ds[:, 128 * n : 128 * n + 128]
        out_ref[:rows, lanes] = jnp.where(half_lanes(dq[0].shape, 0), dq[0], dq[1]).astype(BF)
        out_ref[rows : rows + length, lanes] = dk.astype(BF)
        out_ref[rows + length :, lanes] = dv.astype(BF)
    if causal:
        for head in range(2 * pairs):
            sums_ref[head] = diagonal_sums(line_ref[head])


def attend_back(place, query, keys, values, grads, bias=None):
    causal = bias is not None
    rows, length = query.shape[0], keys.shape[0]
    pairs = 2 if causal else 6
    wide = 128 * pairs
    total = rows + 2 * length
    some = pl.BlockSpec((rows, wide), lambda p: (0, p))
    every = pl.BlockSpec((length, wide), lambda p: (0, p))
    in_specs = [pl.BlockSpec(memory_space=pltpu.SMEM), some, every, every, some]
    out_specs = [pl.BlockSpec((total, wide), lambda p: (0, p))]
    out_shape = [jax.ShapeDtypeStruct((total, 768), BF)]
    scratch = []
    if causal:
        in_specs.append(pl.BlockSpec((2 * pairs, 8, 128, 128), lambda p: (p, 0, 0, 0)))
        out_specs.append(pl.BlockSpec((2 * pairs, 1, length + 128), lambda p: (p, 0, 0)))
        out_shape.append(jax.ShapeDtypeStruct((HEADS, 1, length + 128), F32))
        scratch.append(pltpu.VMEM((2 * pairs, rows, length + 128), F32))
    return pl.pallas_call(
        functools.partial(backward_kernel, causal, pairs),
        grid=(PAIRS // pairs,),
        in_specs=in_specs,
        out_specs=out_specs,
        out_shape=out_shape,
        scratch_shapes=scratch,
        compiler_params=PARAMS,
        cost_estimate=cost(14.5 if causal else 7),
        name="self_backward" if causal else "cross_backward",
    )(place, query, keys, values, grads, *((bias,) if causal else ()))


def body(
    inputs,
    encoded,
    cotangent,
    buckets,
    bias_table,
    norm_self,
    norm_cross,
    norm_feed,
    self_query,
    self_key,
    self_value,
    self_out,
    cross_query,
    cross_key,
    cross_value,
    cross_out,
    feed_gate,
    feed_up,
    feed_down,
):
    core = lax.axis_index("c")
    place_x = lax.axis_index("x")
    place = jnp.stack([place_x * 2 + core, core, place_x]).astype(jnp.int32)

    packed_cross = packed_rows((cross_query, cross_key, cross_value, cross_out))

    def by_owner(w):
        return w.reshape(6, 16, 8, 16).transpose(2, 0, 1, 3).reshape(8, 6, 256)

    gate_up = jnp.concatenate([by_owner(feed_gate), by_owner(feed_up)], axis=2)
    gate_up = after(gate_up, packed_cross)
    packed_cross = lax.all_gather(packed_cross, ALL, axis=0, tiled=True)
    gate_up_sent = exchange(gate_up, SEQ).reshape(48, 512)

    packed_self = packed_rows(
        (self_query, self_key, self_value, self_out), (norm_self, norm_cross, norm_feed)
    )
    packed_self = copies(after(packed_self, gate_up_sent), CHIPS, 64).reshape(2048, 768)

    first = jnp.concatenate([inputs[0], encoded[0]], axis=0)
    first_own, first_other = around_x(first)
    first_own, first_other = first_own.reshape(4, 160, 768), first_other.reshape(4, 160, 768)
    cot = cotangent[0]

    ids = jnp.arange(32, dtype=jnp.int32)
    flipped = jnp.concatenate([buckets[::-1], jnp.full((128,), -1, jnp.int32)])
    hits = (flipped[None, :] == ids[:, None]).astype(BF)
    line = dot(bias_table.T, hits)
    tiles = bias_tiles(line.reshape(HEADS, 1, 1152))

    feed = jnp.concatenate(
        [gate_up_sent, feed_down[:, :512], jnp.pad(feed_down[:, 512:], ((0, 0), (0, 256)))], axis=0
    )
    feed = gathered(after(feed, first_own), "z").reshape(320, 512)
    cot_own, cot_other = around_x(after(cot, first_own))
    states = jnp.concatenate([first_own[:, 128:], first_other[:, 128:]], axis=0).reshape(256, 768)

    f = jnp.arange(768, dtype=jnp.int32)
    n = jnp.arange(384, dtype=jnp.int32)
    pick = (f[:, None] == (n // 6 * 12 + 6 * core + n % 6)[None, :]).astype(BF)

    def picked(a):
        return dot(a, pick).astype(BF)

    low_states = picked(states)

    flipped = jnp.concatenate(
        [jnp.full((128,), -1, jnp.int32), flipped[:1024], jnp.full((1024,), -1, jnp.int32)]
    )
    start = 1151 - 128 * place[0]
    around = jnp.concatenate(
        [
            lax.dynamic_slice(flipped, (start,), (1024,)),
            lax.dynamic_slice(flipped, (start - 128,), (128,)),
        ]
    )
    table_hits = (around[:, None] == ids[None, :]).astype(F32)

    (
        packed_self, first_own, first_other, states, low_states, tiles, table_hits, pick, feed, cot_own, cot_other,
    ) = lax.optimization_barrier(
        (packed_self, first_own, first_other, states, low_states, tiles, table_hits, pick, feed, cot_own, cot_other)
    )

    w_q, w_k, w_v, w_o, gains = unpack_cores(core, packed_self, other_core(packed_self))
    gains = gains[:, :3].astype(F32).T
    gain_self, gain_cross, gain_feed = gains[0:1], gains[1:2], gains[2:3]

    x = inputs[0].astype(F32)
    x_all = jnp.concatenate([first_own[:, :128], first_other[:, :128]], axis=0)
    x_all = x_all.reshape(1024, 768).astype(F32)

    hat_all, _ = normed(x_all)
    low_all = (hat_all * gain_self).astype(BF)
    hat_one, r_one = normed(x)
    low_one = (hat_one * gain_self).astype(BF)
    query = dot(low_one, w_q).astype(BF)
    keys = dot(low_all, w_k).astype(BF)
    values = dot(low_all, w_v).astype(BF)
    feed = gathered(after(feed, keys), "y").reshape(16, 80, 512)
    mixed = attend(place, query, keys, values, tiles)
    feed = after(feed, mixed)
    gate_up = feed[:, :48].reshape(768, 512)
    down = jnp.concatenate([feed[:, 48:64], feed[:, 64:, :256]], axis=2).reshape(256, 768)
    after_self = x + dot(mixed, w_o)
    c_q, c_k, c_v, c_o = unpack_four(after(packed_cross, mixed))
    hat_two, r_two = normed(after_self)
    low_two = (hat_two * gain_cross).astype(BF)
    query_two = dot(low_two, c_q).astype(BF)
    keys_two = dot(states, c_k).astype(BF)
    values_two = dot(states, c_v).astype(BF)
    mixed_two = attend(place, query_two, keys_two, values_two)
    after_cross = after_self + dot(mixed_two, c_o)
    hat_three, r_three = normed(after_cross)
    low_three = (hat_three * gain_feed).astype(BF)

    def feed_half(low, cot_half):
        both = dot(low, gate_up)
        gate, upper = both[:, :256], both[:, 256:]
        tanh = jnp.tanh(0.7978845608028654 * (gate + 0.044715 * gate * gate * gate))
        gelu_gate = 0.5 * gate * (1.0 + tanh)
        slope = 0.5 * (1.0 + tanh) + 0.5 * gate * (1.0 - tanh * tanh) * (
            0.7978845608028654 * (1.0 + 3.0 * 0.044715 * gate * gate)
        )
        hidden = (gelu_gate * upper).astype(BF)
        grad_hidden = dot_t(cot_half, down)
        low_gate = (grad_hidden * upper * slope).astype(BF)
        low_upper = (grad_hidden * gelu_gate).astype(BF)
        low_both = jnp.concatenate([low_gate, low_upper], axis=1)
        part_three = dot_t(low_both, gate_up).astype(BF)
        return hidden, low_both, part_three

    low_own, low_other = around_x(low_three)
    hidden_a, both_a, three_a = feed_half(low_own, cot_own)
    hidden_b, both_b, three_b = feed_half(low_other, cot_other)
    grad_low_three = to_owner(three_a, three_b)
    out_a = dot(hidden_a, down).astype(BF)
    out_b = dot(hidden_b, down).astype(BF)
    d_both = (t_dot(low_own, both_a) + t_dot(low_other, both_b)).astype(BF).reshape(16, 48, 512)
    d_down = (t_dot(hidden_a, cot_own) + t_dot(hidden_b, cot_other)).astype(BF).reshape(16, 16, 768)
    d_feed = jnp.concatenate(
        [d_both, d_down[:, :, :512], jnp.pad(d_down[:, :, 512:], ((0, 0), (0, 0), (0, 256)))], axis=1
    )
    grad_low_three, out_a, out_b, d_feed = lax.optimization_barrier(
        (grad_low_three, out_a, out_b, d_feed)
    )
    output = (after_cross + to_owner(out_a, out_b)).astype(BF)[None]
    d_feed = jnp.sum(exchange(d_feed, ROWS).astype(F32), axis=0)
    d_down = jnp.concatenate([d_feed[48:64], d_feed[64:80, :256]], axis=1)
    d_both = exchange(d_feed[:48].reshape(8, 6, 512), SEQ)

    def to_columns(part):
        return part.reshape(8, 6, 16, 16).transpose(1, 2, 0, 3).reshape(6, 2048)


    g_norm_feed = jnp.sum(grad_low_three * hat_three, axis=0)
    grad_two = cot.astype(F32) + norm_back(grad_low_three, hat_three, r_three, gain_feed)

    low_cross = grad_two.astype(BF)
    grad_mixed_two = dot_t(low_cross, c_o).astype(BF)
    (back_two,) = attend_back(place, query_two, keys_two, values_two, grad_mixed_two)
    back_two = after(back_two, d_feed)
    grad_low_two = dot_t(back_two[:128], c_q)
    g_norm_cross = jnp.sum(grad_low_two * hat_two, axis=0)
    grad_one = grad_two + norm_back(grad_low_two, hat_two, r_two, gain_cross)
    low_self = grad_one.astype(BF)

    def summed(a, b):
        half = a.shape[0] // 2
        b = jnp.concatenate([b[half:], b[:half]], axis=0)
        return (a.astype(F32) + b.astype(F32)).astype(BF)

    def both_cores(left, grads, left_other, grads_other):
        return (t_dot(left, grads) + t_dot(left_other, grads_other)).astype(BF)

    mine = jnp.concatenate([low_two, mixed_two, low_cross], axis=0)
    theirs = other_core(mine)
    back_other = other_core(back_two)
    dk_two = summed(back_two[128:384], back_other[128:384])
    dv_two = summed(back_two[384:], back_other[384:])
    left, left_other = picked(mine[:256]), picked(theirs[:256])
    d_cross = pack(
        [
            both_cores(left[:128], back_two[:128], left_other[:128], back_other[:128]),
            t_dot(low_states, dk_two).astype(BF),
            t_dot(low_states, dv_two).astype(BF),
            both_cores(left[128:], low_cross, left_other[128:], theirs[256:]),
        ]
    )
    part_states = (dot_t(dk_two[:128], c_k) + dot_t(dv_two[:128], c_v)).astype(BF)

    grad_mixed = dot_t(low_self, w_o).astype(BF)
    mine = jnp.concatenate([low_one, mixed, low_self], axis=0)
    theirs = other_core(mine)
    left, left_other = picked(mine[:256]), picked(theirs[:256])
    low_picked = picked(low_all)
    grad_mixed, d_cross, part_states, low_picked, left, left_other = lax.optimization_barrier(
        (grad_mixed, d_cross, part_states, low_picked, left, left_other)
    )
    d_cross = exchange(after(d_cross, d_both), CHIPS)
    grad_mixed = after(grad_mixed, d_both)
    back, sums = attend_back(place, query, keys, values, grad_mixed, tiles)
    back_other = other_core(back)
    dq = back[:128]
    dk = summed(back[128:1152], back_other[128:1152])
    dv = summed(back[1152:], back_other[1152:])
    part_one = dot_t(dk[:512], w_k) + dot_t(dv[:512], w_v)
    own_one = dot_t(dq, w_q)
    g_norm_self = jnp.sum(part_one * hat_all[:512], axis=0) + jnp.sum(own_one * hat_one, axis=0)

    table = lax.dot_general(
        table_hits, sums.reshape(HEADS, 1152), (((0,), (1,)), ((), ())), precision=lax.Precision.HIGHEST
    )
    scales = jnp.stack([g_norm_self, g_norm_cross, g_norm_feed])
    table, scales = table + other_core(table), scales + other_core(scales)
    scales = scales.reshape(3, 64, 12)
    scales = jnp.pad(scales.transpose(1, 0, 2), ((0, 0), (0, 0), (0, 116)))
    small = jnp.concatenate([scales, jnp.broadcast_to(table.reshape(1, 3, 128), (64, 3, 128))], axis=1)
    high = lax.reduce_precision(small, 8, 7)
    rest = (small - high).astype(BF)
    extra = jnp.concatenate([high.astype(BF), rest, jnp.zeros((64, 12, 128), BF)], axis=1)

    parts = jnp.concatenate(
        [part_one.astype(BF).reshape(4, 128, 768), part_states.reshape(4, 32, 768)], axis=1
    )
    arrived = back_around_x(parts.reshape(640, 768))
    grad_low_one = own_one + arrived[:128]
    grad_encoded = arrived[128:][None]
    grad_inputs = (grad_one + norm_back(grad_low_one, hat_one, r_one, gain_self))[None]
    d_self = pack(
        [
            both_cores(left[:128], dq, left_other[:128], back_other[:128]),
            t_dot(low_picked, dk).astype(BF),
            t_dot(low_picked, dv).astype(BF),
            both_cores(left[128:], low_self, left_other[128:], theirs[256:]),
        ],
        extra,
    )
    d_self = jnp.sum(exchange(after(d_self, d_cross), CHIPS).astype(F32), axis=0)
    d_cross = jnp.sum(d_cross.astype(F32), axis=0)
    d_gate, d_up = to_columns(d_both[:, :, :256]), to_columns(d_both[:, :, 256:])

    small = d_self[:6, 768:] + d_self[6:12, 768:]
    table_grad = small[3:6].reshape(32, 12)
    scales = jnp.where(core == 0, small[:3, :6], small[:3, 6:12])
    d_self = d_self[:, :768]

    return (
        output,
        grad_inputs,
        grad_encoded,
        table_grad,
        scales[0],
        scales[1],
        scales[2],
        d_self[0:6],
        d_self[6:12],
        d_self[12:18],
        d_self[18:24],
        d_cross[0:6],
        d_cross[6:12],
        d_cross[12:18],
        d_cross[18:24],
        d_gate,
        d_up,
        d_down,
    )


def solution(mesh):
    finer = Mesh(mesh.devices.reshape(4, 4, 4, 2), ALL)
    tokens = P(ROWS, SEQ, None)
    scale, weight = P(ALL), P(ALL, None)
    return jax.shard_map(
        body,
        mesh=finer,
        in_specs=(tokens, tokens, tokens, P(), P(), *([scale] * 3), *([weight] * 11)),
        out_specs=(tokens, tokens, tokens, P(), *([scale] * 3), *([weight] * 11)),
        check_vma=False,
    )
```

```python
import functools

import jax
import jax.numpy as jnp
from jax import lax
from jax.experimental import pallas as pl
from jax.experimental.pallas import tpu as pltpu
from jax.sharding import Mesh
from jax.sharding import PartitionSpec as P

HEADS = 12
PAIRS = HEADS // 2
EPS = 1e-06
MASKED = -1e30
BF = jnp.bfloat16
F32 = jnp.float32
ALL = ("y", "z", "x", "c")
CHIPS = ("y", "z", "x")
ROWS = ("y", "z")
SEQ = ("x", "c")
SWAP = [(0, 1), (1, 0)]
PARAMS = pltpu.CompilerParams(vmem_limit_bytes=56 * 1024 * 1024)


def other_core(a):
    return lax.ppermute(a, "c", SWAP)


def exchange(a, axes):
    return lax.all_to_all(a, axes, 0, 0, tiled=True)


def copies(a, axes, count):
    return exchange(jnp.broadcast_to(a[None], (count, *a.shape)), axes)


def shifted(a, by):
    return lax.ppermute(a, "x", [((i + by) % 4, i) for i in range(4)])


def around_x(a):
    own = jnp.concatenate([a, *(shifted(a, by) for by in (1, 2, 3))], axis=0)
    return own, other_core(own)


def gathered(a, axis):
    place = lax.axis_index(axis)
    whole = jnp.zeros((4, *a.shape), a.dtype)
    for by in range(4):
        part = a
        if by:
            part = lax.ppermute(a, axis, [((i + by) % 4, i) for i in range(4)])
        whole = lax.dynamic_update_index_in_dim(whole, part, lax.rem(place + by, 4), 0)
    return whole


def back_around_x(parts, *earlier):
    rows = parts.shape[0] // 4
    own, *others = [parts[rows * n : rows * n + rows] for n in range(4)]
    others = [shifted(a, -by) for by, a in enumerate(others, 1)]
    if earlier:
        others = lax.optimization_barrier((*others, *earlier))[:3]
    return own.astype(F32) + sum(a.astype(F32) for a in others)


def core_sum(own, other):
    return (own.astype(F32) + other_core(other).astype(F32)).astype(BF)


def after(a, *earlier):
    return lax.optimization_barrier((a, *earlier))[0]


def cost(us):
    return pl.CostEstimate(flops=int(us * 1.0e9), bytes_accessed=int(us * 1.0e6), transcendentals=0)


def dot(a, b):
    return jnp.dot(a, b, preferred_element_type=F32)


def dot_t(a, b):
    return lax.dot_general(a, b, (((1,), (1,)), ((), ())), preferred_element_type=F32)


def t_dot(a, b):
    return lax.dot_general(a, b, (((0,), (0,)), ((), ())), preferred_element_type=F32)


def normed(v):
    r = lax.rsqrt(jnp.mean(v * v, axis=-1, keepdims=True) + EPS)
    return v * r, r


def norm_back(g, hat, r, gain):
    scaled = g * gain
    return r * (scaled - hat * jnp.mean(scaled * hat, axis=-1, keepdims=True))


def gelu(v):
    return 0.5 * v * (1.0 + jnp.tanh(0.7978845608028654 * (v + 0.044715 * v * v * v)))


def gather_rows_kernel(count, *refs):
    weights, out, rows = refs[:count], refs[-2], refs[-1]
    rows[...] = jnp.zeros_like(rows)
    for m, w in enumerate(weights):
        rows[6 * m : 6 * m + 6] = w[...].astype(F32)
    if len(refs) == count + 3:
        row = lax.broadcasted_iota(jnp.int32, (8, 128), 0)
        lane = lax.broadcasted_iota(jnp.int32, (8, 128), 1)
        unit = (row == lane).astype(F32)
        wide = jnp.concatenate([refs[count][...], jnp.zeros((120, 128), F32)], axis=0)
        rows[6 * count : 6 * count + 6, :128] = dot_t(unit, wide)[:6]
    out[...] = rows[...].astype(BF)


def packed_rows(weights, norms=()):
    count = len(weights)
    total = -(-(6 * count + (6 if norms else 0)) // 8) * 8
    more = [jnp.pad(jnp.stack(norms).astype(F32), ((0, 5), (0, 122)))] if norms else []
    return pl.pallas_call(
        functools.partial(gather_rows_kernel, count),
        out_shape=jax.ShapeDtypeStruct((total, 768), BF),
        scratch_shapes=[pltpu.VMEM((total, 768), F32)],
        compiler_params=PARAMS,
        cost_estimate=cost(2),
        name="packed_rows",
    )(*weights, *more)


def unpack_all_kernel(place_ref, packed_ref, *outs):
    for b in range(4):
        halves = [
            dot(place_ref[...], packed_ref[256 * b + 128 * n : 256 * b + 128 * n + 128])
            for n in range(2)
        ]
        for m, out in enumerate(outs):
            rows = jnp.concatenate([h[24 * m : 24 * m + 24] for h in halves], axis=0)
            out[48 * b : 48 * b + 48] = rows.astype(BF)


def unpack_all(packed):
    q = jnp.arange(120, dtype=jnp.int32)
    source = (q % 24) // 6 * 32 + q // 24 * 6 + q % 6
    place = (source[:, None] == jnp.arange(128, dtype=jnp.int32)[None, :]).astype(BF)
    return pl.pallas_call(
        unpack_all_kernel,
        grid=(4,),
        in_specs=[
            pl.BlockSpec((120, 128), lambda b: (0, 0)),
            pl.BlockSpec((1024, 768), lambda b: (b, 0)),
        ],
        out_specs=[pl.BlockSpec((192, 768), lambda b: (b, 0))] * 5,
        out_shape=[jax.ShapeDtypeStruct((768, 768), BF)] * 5,
        compiler_params=PARAMS,
        cost_estimate=cost(6),
        name="unpack_all",
    )(place, packed)


def unpack_cores_kernel(place_ref, mine_ref, theirs_ref, *outs):
    for b in range(4):
        at = slice(96 * b, 96 * b + 96)
        whole = dot(place_ref[...], jnp.concatenate([mine_ref[at], theirs_ref[at]], axis=0))
        for m, out in enumerate(outs):
            out[48 * b : 48 * b + 48] = whole[48 * m : 48 * m + 48, : out.shape[1]].astype(BF)


def unpack_cores(core, mine, theirs):
    q = jnp.arange(192, dtype=jnp.int32)
    device, row = (q % 48) // 6, q // 48 * 6 + q % 6
    source = (device % 2 ^ core) * 96 + device // 2 * 24 + row
    place = (source[:, None] == q[None, :]).astype(BF)
    widths = (768, 768, 768, 128)
    return pl.pallas_call(
        unpack_cores_kernel,
        grid=(4,),
        in_specs=[
            pl.BlockSpec((192, 192), lambda b: (0, 0)),
            pl.BlockSpec((384, 768), lambda b: (b, 0)),
            pl.BlockSpec((384, 768), lambda b: (b, 0)),
        ],
        out_specs=[pl.BlockSpec((192, w), lambda b: (b, 0)) for w in widths],
        out_shape=[jax.ShapeDtypeStruct((768, w), BF) for w in widths],
        compiler_params=PARAMS,
        cost_estimate=cost(6),
        name="unpack_cores",
    )(place, mine, theirs)


def weight_grads_kernel(
    place_ref, own_ref, other_ref, tokens_ref, dq_ref, dq_other_ref, dk_ref, dv_ref, out_own_ref, out_other_ref, *rest
):
    out_ref = rest[-1]
    n = pl.program_id(0)
    four = [
        dot(own_ref[:, :128], dq_ref[...]) + dot(other_ref[:, :128], dq_other_ref[...]),
        dot(tokens_ref[...], dk_ref[...]),
        dot(tokens_ref[...], dv_ref[...]),
        dot(own_ref[:, 128:], out_own_ref[...]) + dot(other_ref[:, 128:], out_other_ref[...]),
    ]
    four = [w.astype(BF) for w in four]
    columns = pl.ds(pl.multiple_of(n * 256, 256), 256)
    for b in range(8):
        rows = jnp.concatenate([w[48 * b : 48 * b + 48] for w in four], axis=0)
        out_ref[192 * b : 192 * b + 192, columns] = dot(place_ref[...], rows).astype(BF)
    if len(rest) == 2:

        @pl.when(n == 0)
        def _():
            out_ref[:, 768:] = rest[0][...]


def weight_grads(own, other, tokens, back, back_other, dk, dv, low, low_other, extra=None):
    p = jnp.arange(192, dtype=jnp.int32)
    source = (p % 24) // 6 * 48 + p // 24 * 6 + p % 6
    place = (source[:, None] == p[None, :]).astype(BF)
    width = 768 if extra is None else 896
    more = [] if extra is None else [extra.reshape(1536, 128)]
    whole = lambda a: pl.BlockSpec(a.shape, lambda n: (0, 0))
    first = pl.BlockSpec((128, 256), lambda n: (0, n))
    every = pl.BlockSpec((dk.shape[0], 256), lambda n: (0, n))
    return pl.pallas_call(
        weight_grads_kernel,
        grid=(3,),
        in_specs=[whole(place), whole(own), whole(other), whole(tokens), first, first, every, every, first, first]
        + [whole(a) for a in more],
        out_specs=pl.BlockSpec((1536, width), lambda n: (0, 0)),
        out_shape=jax.ShapeDtypeStruct((1536, width), BF),
        compiler_params=PARAMS,
        cost_estimate=cost(5),
        name="weight_grads",
    )(place, own, other, tokens, back, back_other, dk, dv, low, low_other, *more).reshape(64, 24, width)


def bias_kernel(line_ref, out_ref):
    for k in range(8):
        segment = line_ref[0, :, 128 * (7 - k) : 128 * (7 - k) + 256]
        wide = jnp.broadcast_to(segment, (128, 256))
        tile = pltpu.roll(wide, 129, 1, stride=1, stride_axis=0)
        out_ref[0, k] = tile[:, :128].astype(BF)


def bias_tiles(line):
    return pl.pallas_call(
        bias_kernel,
        grid=(HEADS,),
        in_specs=[pl.BlockSpec((1, 1, 1152), lambda h: (h, 0, 0))],
        out_specs=pl.BlockSpec((1, 8, 128, 128), lambda h: (h, 0, 0, 0)),
        out_shape=jax.ShapeDtypeStruct((HEADS, 8, 128, 128), BF),
        compiler_params=PARAMS,
        cost_estimate=cost(7.5),
        name="bias_tiles",
    )(line)


def half_lanes(shape, half):
    lane = lax.broadcasted_iota(jnp.int32, shape, 1)
    return (lane >= 64) if half else (lane < 64)


def block_offsets(place_ref):
    s, c, x = place_ref[0], place_ref[1], place_ref[2]
    return [
        s - (2 * lax.rem(x + n, 4) + (c if e == 0 else 1 - c)) for e in range(2) for n in range(4)
    ]


def add_bias(raw, bias_ref, half, away):
    i = lax.broadcasted_iota(jnp.int32, (128, 128), 0)
    j = lax.broadcasted_iota(jnp.int32, (128, 128), 1)
    parts = []
    for n, k in enumerate(away):
        tile = bias_ref[half, jnp.clip(k, 0, 7)].astype(F32)
        parts.append(
            jnp.where(i - j + 128 * k >= 0, raw[:, 128 * n : 128 * n + 128] + tile, MASKED)
        )
    return jnp.concatenate(parts, axis=1)


def forward_kernel(causal, pairs, place_ref, q_ref, k_ref, v_ref, *rest):
    bias_ref, out_ref = rest if causal else (None, rest[0])
    away = block_offsets(place_ref) if causal else None
    for pair in range(pairs):
        lanes = slice(128 * pair, 128 * pair + 128)
        keys, values, query = k_ref[:, lanes], v_ref[:, lanes], q_ref[:, lanes]
        mixed = []
        for half in range(2):
            low = half_lanes(query.shape, half)
            scores = dot_t(jnp.where(low, query, jnp.zeros_like(query)), keys)
            if causal:
                scores = add_bias(scores, bias_ref, 2 * pair + half, away)
            parts = jnp.exp(scores - jnp.max(scores, axis=-1, keepdims=True))
            share = 1.0 / jnp.sum(parts, axis=-1, keepdims=True)
            mixed.append(dot(parts.astype(BF), values) * share)
        out_ref[:, lanes] = jnp.where(half_lanes(mixed[0].shape, 0), mixed[0], mixed[1]).astype(BF)


def attend(place, query, keys, values, bias=None):
    causal = bias is not None
    rows, length = query.shape[0], keys.shape[0]
    pairs = 2 if causal else 6
    wide = 128 * pairs
    in_specs = [
        pl.BlockSpec(memory_space=pltpu.SMEM),
        pl.BlockSpec((rows, wide), lambda p: (0, p)),
        pl.BlockSpec((length, wide), lambda p: (0, p)),
        pl.BlockSpec((length, wide), lambda p: (0, p)),
    ]
    if causal:
        in_specs.append(pl.BlockSpec((2 * pairs, 8, 128, 128), lambda p: (p, 0, 0, 0)))
    return pl.pallas_call(
        functools.partial(forward_kernel, causal, pairs),
        grid=(PAIRS // pairs,),
        in_specs=in_specs,
        out_specs=pl.BlockSpec((rows, wide), lambda p: (0, p)),
        out_shape=jax.ShapeDtypeStruct((rows, 768), BF),
        compiler_params=PARAMS,
        cost_estimate=cost(7.5 if causal else 3),
        name="self_forward" if causal else "cross_forward",
    )(place, query, keys, values, *((bias,) if causal else ()))


def diagonal_sums(t):
    rows, width = t.shape
    while rows > 8:
        rows //= 2
        t = t[:rows] + pltpu.roll(t[rows:], width - rows, 1)
    row = lax.broadcasted_iota(jnp.int32, t.shape, 0)
    for step in (4, 2, 1):
        t = jnp.where((row & step) != 0, pltpu.roll(t, width - step, 1), t)
    return jnp.sum(t, axis=0, keepdims=True)


def backward_kernel(causal, pairs, place_ref, q_ref, k_ref, v_ref, g_ref, *rest):
    rows, length = q_ref.shape[0], k_ref.shape[0]
    if causal:
        bias_ref, out_ref, sums_ref, line_ref = rest
        away = block_offsets(place_ref)
        line_ref[:, :, length:] = jnp.zeros((2 * pairs, rows, 128), F32)
    else:
        (out_ref,) = rest
    for pair in range(pairs):
        lanes = slice(128 * pair, 128 * pair + 128)
        keys, values, query, grads = k_ref[:, lanes], v_ref[:, lanes], q_ref[:, lanes], g_ref[:, lanes]
        dq, dk, dv = [], 0.0, 0.0
        for half in range(2):
            low = half_lanes(query.shape, half)
            own_query = jnp.where(low, query, jnp.zeros_like(query))
            own_grads = jnp.where(low, grads, jnp.zeros_like(grads))
            scores = dot_t(own_query, keys)
            if causal:
                scores = add_bias(scores, bias_ref, 2 * pair + half, away)
            parts = jnp.exp(scores - jnp.max(scores, axis=-1, keepdims=True))
            shares = parts * (1.0 / jnp.sum(parts, axis=-1, keepdims=True))
            pushed = dot_t(own_grads, values)
            center = jnp.sum(shares * pushed, axis=-1, keepdims=True)
            ds = shares * (pushed - center)
            low_ds = ds.astype(BF)
            dq.append(dot(low_ds, keys))
            dk = dk + t_dot(low_ds, own_query)
            dv = dv + t_dot(shares.astype(BF), own_grads)
            if causal:
                for n, k in enumerate(away):
                    at = pl.multiple_of((place_ref[0] - k) * 128, 128)
                    line_ref[2 * pair + half, :, pl.ds(at, 128)] = ds[:, 128 * n : 128 * n + 128]
        out_ref[:rows, lanes] = jnp.where(half_lanes(dq[0].shape, 0), dq[0], dq[1]).astype(BF)
        out_ref[rows : rows + length, lanes] = dk.astype(BF)
        out_ref[rows + length :, lanes] = dv.astype(BF)
    if causal:
        for head in range(2 * pairs):
            sums_ref[head] = diagonal_sums(line_ref[head])


def attend_back(place, query, keys, values, grads, bias=None):
    causal = bias is not None
    rows, length = query.shape[0], keys.shape[0]
    pairs = 2 if causal else 6
    wide = 128 * pairs
    total = rows + 2 * length
    some = pl.BlockSpec((rows, wide), lambda p: (0, p))
    every = pl.BlockSpec((length, wide), lambda p: (0, p))
    in_specs = [pl.BlockSpec(memory_space=pltpu.SMEM), some, every, every, some]
    out_specs = [pl.BlockSpec((total, wide), lambda p: (0, p))]
    out_shape = [jax.ShapeDtypeStruct((total, 768), BF)]
    scratch = []
    if causal:
        in_specs.append(pl.BlockSpec((2 * pairs, 8, 128, 128), lambda p: (p, 0, 0, 0)))
        out_specs.append(pl.BlockSpec((2 * pairs, 1, length + 128), lambda p: (p, 0, 0)))
        out_shape.append(jax.ShapeDtypeStruct((HEADS, 1, length + 128), F32))
        scratch.append(pltpu.VMEM((2 * pairs, rows, length + 128), F32))
    return pl.pallas_call(
        functools.partial(backward_kernel, causal, pairs),
        grid=(PAIRS // pairs,),
        in_specs=in_specs,
        out_specs=out_specs,
        out_shape=out_shape,
        scratch_shapes=scratch,
        compiler_params=PARAMS,
        cost_estimate=cost(14.5 if causal else 2),
        name="self_backward" if causal else "cross_backward",
    )(place, query, keys, values, grads, *((bias,) if causal else ()))


def body(
    inputs,
    encoded,
    cotangent,
    buckets,
    bias_table,
    norm_self,
    norm_cross,
    norm_feed,
    self_query,
    self_key,
    self_value,
    self_out,
    cross_query,
    cross_key,
    cross_value,
    cross_out,
    feed_gate,
    feed_up,
    feed_down,
):
    core = lax.axis_index("c")
    place_x = lax.axis_index("x")
    place = jnp.stack([place_x * 2 + core, core, place_x]).astype(jnp.int32)

    packed_cross = packed_rows((cross_query, cross_key, cross_value, cross_out, self_out))

    def by_owner(w):
        return w.reshape(6, 16, 8, 16).transpose(2, 0, 1, 3).reshape(8, 6, 256)

    gate_up = jnp.concatenate([by_owner(feed_gate), by_owner(feed_up)], axis=2)
    gate_up = after(gate_up, packed_cross)
    packed_cross = lax.all_gather(packed_cross, ALL, axis=0, tiled=True)
    gate_up_sent = exchange(gate_up, SEQ).reshape(48, 512)

    packed_self = packed_rows(
        (self_query, self_key, self_value), (norm_self, norm_cross, norm_feed)
    )
    packed_self = jnp.broadcast_to(packed_self[None], (64, 24, 768))
    packed_self = sent_self = after(packed_self, gate_up_sent)
    packed_self = exchange(packed_self, CHIPS).reshape(1536, 768)

    first = jnp.concatenate([inputs[0], encoded[0]], axis=0)
    first_own, first_other = around_x(first)
    first_own, first_other = first_own.reshape(4, 160, 768), first_other.reshape(4, 160, 768)
    cot = cotangent[0]

    ids = jnp.arange(32, dtype=jnp.int32)
    flipped = jnp.concatenate([buckets[::-1], jnp.full((128,), -1, jnp.int32)])
    hits = (flipped[None, :] == ids[:, None]).astype(BF)
    line = dot(bias_table.T, hits)
    tiles = bias_tiles(after(line, sent_self).reshape(HEADS, 1, 1152))

    feed = jnp.concatenate(
        [gate_up_sent, feed_down[:, :512], jnp.pad(feed_down[:, 512:], ((0, 0), (0, 256)))], axis=0
    )
    feed = gathered(after(feed, first_own), "z").reshape(320, 512)
    cot_own, cot_other = around_x(after(cot, first_own))
    states = jnp.concatenate([first_own[:, 128:], first_other[:, 128:]], axis=0).reshape(256, 768)

    f = jnp.arange(768, dtype=jnp.int32)
    n = jnp.arange(384, dtype=jnp.int32)
    pick = (f[None, :] == (n // 6 * 12 + 6 * core + n % 6)[:, None]).astype(BF)

    def picked(a):
        return dot_t(pick, a).astype(BF)

    low_states = picked(states)

    flipped = jnp.concatenate(
        [jnp.full((128,), -1, jnp.int32), flipped[:1024], jnp.full((1024,), -1, jnp.int32)]
    )
    start = 1151 - 128 * place[0]
    around = jnp.concatenate(
        [
            lax.dynamic_slice(flipped, (start,), (1024,)),
            lax.dynamic_slice(flipped, (start - 128,), (128,)),
        ]
    )
    table_hits = (around[:, None] == ids[None, :]).astype(F32)

    (
        packed_self, first_own, first_other, states, low_states, tiles, table_hits, pick, feed, cot_own, cot_other,
    ) = lax.optimization_barrier(
        (packed_self, first_own, first_other, states, low_states, tiles, table_hits, pick, feed, cot_own, cot_other)
    )

    w_q, w_k, w_v, gains = unpack_cores(core, packed_self, other_core(packed_self))
    gains = gains[:, :3].astype(F32).T
    gain_self, gain_cross, gain_feed = gains[0:1], gains[1:2], gains[2:3]

    x = inputs[0].astype(F32)
    x_all = jnp.concatenate([first_own[:, :128], first_other[:, :128]], axis=0)
    x_all = x_all.reshape(1024, 768).astype(F32)

    hat_all, _ = normed(x_all)
    low_all = (hat_all * gain_self).astype(BF)
    hat_one, r_one = normed(x)
    low_one = (hat_one * gain_self).astype(BF)
    query = dot(low_one, w_q).astype(BF)
    keys = dot(low_all, w_k).astype(BF)
    values = dot(low_all, w_v).astype(BF)
    feed = gathered(after(feed, keys), "y").reshape(16, 80, 512)
    mixed = attend(place, query, keys, values, tiles)
    feed = after(feed, mixed)
    gate_up = feed[:, :48].reshape(768, 512)
    down = jnp.concatenate([feed[:, 48:64], feed[:, 64:, :256]], axis=2).reshape(256, 768)
    c_q, c_k, c_v, c_o, w_o = unpack_all(after(packed_cross, mixed))
    after_self = x + dot(mixed, w_o)
    hat_two, r_two = normed(after_self)
    low_two = (hat_two * gain_cross).astype(BF)
    query_two = dot(low_two, c_q).astype(BF)
    keys_two = dot(states, c_k).astype(BF)
    values_two = dot(states, c_v).astype(BF)
    mixed_two = attend(place, query_two, keys_two, values_two)
    after_cross = after_self + dot(mixed_two, c_o)
    hat_three, r_three = normed(after_cross)
    low_three = (hat_three * gain_feed).astype(BF)

    left_self = jnp.concatenate([low_one, mixed], axis=0)
    left_cross = jnp.concatenate([low_two, mixed_two], axis=0)
    other_self, other_cross = other_core(left_self), other_core(left_cross)
    left_self, left_cross, other_self, other_cross = (
        picked(after(a, low_three)) for a in (left_self, left_cross, other_self, other_cross)
    )
    low_picked = picked(after(low_all, low_three))

    def feed_half(low, cot_half):
        both = dot(low, gate_up)
        gate, upper = both[:, :256], both[:, 256:]
        tanh = jnp.tanh(0.7978845608028654 * (gate + 0.044715 * gate * gate * gate))
        gelu_gate = 0.5 * gate * (1.0 + tanh)
        slope = 0.5 * (1.0 + tanh) + 0.5 * gate * (1.0 - tanh * tanh) * (
            0.7978845608028654 * (1.0 + 3.0 * 0.044715 * gate * gate)
        )
        hidden = (gelu_gate * upper).astype(BF)
        grad_hidden = dot_t(cot_half, down)
        low_gate = (grad_hidden * upper * slope).astype(BF)
        low_upper = (grad_hidden * gelu_gate).astype(BF)
        low_both = jnp.concatenate([low_gate, low_upper], axis=1)
        part_three = dot_t(low_both, gate_up).astype(BF)
        return hidden, low_both, part_three

    low_own, low_other = around_x(low_three)
    hidden_a, both_a, three_a = feed_half(low_own, cot_own)
    hidden_b, both_b, three_b = feed_half(low_other, cot_other)
    grad_low_three = back_around_x(core_sum(three_a, three_b))
    out_a = dot(hidden_a, down).astype(BF)
    out_b = dot(hidden_b, down).astype(BF)
    d_both = (t_dot(low_own, both_a) + t_dot(low_other, both_b)).astype(BF).reshape(16, 48, 512)
    d_down = (t_dot(hidden_a, cot_own) + t_dot(hidden_b, cot_other)).astype(BF).reshape(16, 16, 768)
    d_feed = jnp.concatenate(
        [d_both, d_down[:, :, :512], jnp.pad(d_down[:, :, 512:], ((0, 0), (0, 0), (0, 256)))], axis=1
    )
    part_out = core_sum(out_a, out_b)
    grad_low_three, part_out, left_self, left_cross, other_self, other_cross, low_picked = lax.optimization_barrier(
        (grad_low_three, part_out, left_self, left_cross, other_self, other_cross, low_picked)
    )
    output = (after_cross + back_around_x(part_out)).astype(BF)[None]
    d_feed = jnp.sum(exchange(d_feed, ROWS).astype(F32), axis=0)
    d_down = jnp.concatenate([d_feed[48:64], d_feed[64:80, :256]], axis=1)
    d_both = exchange(d_feed[:48].reshape(8, 6, 512), SEQ)

    def to_columns(part):
        return part.reshape(8, 6, 16, 16).transpose(1, 2, 0, 3).reshape(6, 2048)


    g_norm_feed = jnp.sum(grad_low_three * hat_three, axis=0)
    grad_two = cot.astype(F32) + norm_back(grad_low_three, hat_three, r_three, gain_feed)

    low_cross = grad_two.astype(BF)
    grad_mixed_two = dot_t(low_cross, c_o).astype(BF)
    (back_two,) = attend_back(place, query_two, keys_two, values_two, grad_mixed_two)
    back_two = after(back_two, d_feed)
    grad_low_two = dot_t(back_two[:128], c_q)
    g_norm_cross = jnp.sum(grad_low_two * hat_two, axis=0)
    grad_one = grad_two + norm_back(grad_low_two, hat_two, r_two, gain_cross)
    low_self = grad_one.astype(BF)

    def summed(a, b):
        half = a.shape[0] // 2
        b = jnp.concatenate([b[half:], b[:half]], axis=0)
        return (a.astype(F32) + b.astype(F32)).astype(BF)

    low_cross_other = other_core(low_cross)
    back_other = other_core(back_two)
    dk_two = summed(back_two[128:384], back_other[128:384])
    dv_two = summed(back_two[384:], back_other[384:])
    d_cross = weight_grads(
        left_cross, other_cross, low_states, back_two, back_other, dk_two, dv_two, low_cross, low_cross_other
    )
    part_states = (dot_t(dk_two[:128], c_k) + dot_t(dv_two[:128], c_v)).astype(BF)

    grad_mixed = dot_t(low_self, w_o).astype(BF)
    low_self_other = other_core(low_self)
    grad_mixed, d_cross, part_states = lax.optimization_barrier((grad_mixed, d_cross, part_states))
    d_cross = exchange(after(d_cross, d_both), CHIPS)
    grad_mixed = after(grad_mixed, d_both)
    back, sums = attend_back(place, query, keys, values, grad_mixed, tiles)
    back, output = lax.optimization_barrier((back, output))
    back_other = other_core(back)
    dq = back[:128]
    dk = summed(back[128:1152], back_other[128:1152])
    dv = summed(back[1152:], back_other[1152:])
    part_one = dot_t(dk[:512], w_k) + dot_t(dv[:512], w_v)
    own_one = dot_t(dq, w_q)
    g_norm_self = jnp.sum(part_one * hat_all[:512], axis=0) + jnp.sum(own_one * hat_one, axis=0)

    table = lax.dot_general(
        table_hits, sums.reshape(HEADS, 1152), (((0,), (1,)), ((), ())), precision=lax.Precision.HIGHEST
    )
    scales = jnp.stack([g_norm_self, g_norm_cross, g_norm_feed])
    table, scales = table + other_core(table), scales + other_core(scales)
    scales = scales.reshape(3, 64, 12)
    scales = jnp.pad(scales.transpose(1, 0, 2), ((0, 0), (0, 0), (0, 116)))
    small = jnp.concatenate([scales, jnp.broadcast_to(table.reshape(1, 3, 128), (64, 3, 128))], axis=1)
    high = lax.reduce_precision(small, 8, 7)
    rest = (small - high).astype(BF)
    extra = jnp.concatenate([high.astype(BF), rest, jnp.zeros((64, 12, 128), BF)], axis=1)

    d_self = weight_grads(
        left_self, other_self, low_picked, back, back_other, dk, dv, low_self, low_self_other, extra
    )

    parts = jnp.concatenate(
        [part_one.astype(BF).reshape(4, 128, 768), part_states.reshape(4, 32, 768)], axis=1
    )
    arrived = back_around_x(parts.reshape(640, 768), d_self)
    grad_low_one = own_one + arrived[:128]
    grad_encoded = arrived[128:][None]
    grad_inputs = (grad_one + norm_back(grad_low_one, hat_one, r_one, gain_self))[None]
    d_self = jnp.sum(exchange(after(d_self, d_cross), CHIPS).astype(F32), axis=0)
    d_cross = jnp.sum(d_cross.astype(F32), axis=0)
    d_gate, d_up = to_columns(d_both[:, :, :256]), to_columns(d_both[:, :, 256:])

    small = d_self[:6, 768:] + d_self[6:12, 768:]
    table_grad = small[3:6].reshape(32, 12)
    scales = jnp.where(core == 0, small[:3, :6], small[:3, 6:12])
    d_self = d_self[:, :768]

    return (
        output,
        grad_inputs,
        grad_encoded,
        table_grad,
        scales[0],
        scales[1],
        scales[2],
        d_self[0:6],
        d_self[6:12],
        d_self[12:18],
        d_self[18:24],
        d_cross[0:6],
        d_cross[6:12],
        d_cross[12:18],
        d_cross[18:24],
        d_gate,
        d_up,
        d_down,
    )


def solution(mesh):
    finer = Mesh(mesh.devices.reshape(4, 4, 4, 2), ALL)
    tokens = P(ROWS, SEQ, None)
    scale, weight = P(ALL), P(ALL, None)
    return jax.shard_map(
        body,
        mesh=finer,
        in_specs=(tokens, tokens, tokens, P(), P(), *([scale] * 3), *([weight] * 11)),
        out_specs=(tokens, tokens, tokens, P(), *([scale] * 3), *([weight] * 11)),
        check_vma=False,
    )
```

```python
import functools

import jax
import jax.numpy as jnp
from jax import lax
from jax.experimental import pallas as pl
from jax.experimental.pallas import tpu as pltpu
from jax.sharding import Mesh
from jax.sharding import PartitionSpec as P

HEADS = 12
PAIRS = HEADS // 2
EPS = 1e-06
MASKED = -1e30
BF = jnp.bfloat16
F32 = jnp.float32
ALL = ("y", "z", "x", "c")
CHIPS = ("y", "z", "x")
ROWS = ("y", "z")
SEQ = ("x", "c")
SWAP = [(0, 1), (1, 0)]
PARAMS = pltpu.CompilerParams(vmem_limit_bytes=56 * 1024 * 1024)


def other_core(a):
    return lax.ppermute(a, "c", SWAP)


def exchange(a, axes):
    return lax.all_to_all(a, axes, 0, 0, tiled=True)


def copies(a, axes, count):
    return exchange(jnp.broadcast_to(a[None], (count, *a.shape)), axes)


def shifted(a, by):
    return lax.ppermute(a, "x", [((i + by) % 4, i) for i in range(4)])


def around_x(a):
    own = jnp.concatenate([a, *(shifted(a, by) for by in (1, 2, 3))], axis=0)
    return own, other_core(own)


def gathered(a, axis):
    place = lax.axis_index(axis)
    whole = jnp.zeros((4, *a.shape), a.dtype)
    for by in range(4):
        part = a
        if by:
            part = lax.ppermute(a, axis, [((i + by) % 4, i) for i in range(4)])
        whole = lax.dynamic_update_index_in_dim(whole, part, lax.rem(place + by, 4), 0)
    return whole


def back_around_x(parts, *earlier):
    rows = parts.shape[0] // 4
    own, *others = [parts[rows * n : rows * n + rows] for n in range(4)]
    others = [shifted(a, -by) for by, a in enumerate(others, 1)]
    if earlier:
        others = lax.optimization_barrier((*others, *earlier))[:3]
    return own.astype(F32) + sum(a.astype(F32) for a in others)


def core_sum(own, other):
    return (own.astype(F32) + other_core(other).astype(F32)).astype(BF)


def after(a, *earlier):
    return lax.optimization_barrier((a, *earlier))[0]


def cost(us):
    return pl.CostEstimate(flops=int(us * 1.0e9), bytes_accessed=int(us * 1.0e6), transcendentals=0)


def dot(a, b):
    return jnp.dot(a, b, preferred_element_type=F32)


def dot_t(a, b):
    return lax.dot_general(a, b, (((1,), (1,)), ((), ())), preferred_element_type=F32)


def t_dot(a, b):
    return lax.dot_general(a, b, (((0,), (0,)), ((), ())), preferred_element_type=F32)


def normed(v):
    r = lax.rsqrt(jnp.mean(v * v, axis=-1, keepdims=True) + EPS)
    return v * r, r


def norm_back(g, hat, r, gain):
    scaled = g * gain
    return r * (scaled - hat * jnp.mean(scaled * hat, axis=-1, keepdims=True))


def gelu(v):
    return 0.5 * v * (1.0 + jnp.tanh(0.7978845608028654 * (v + 0.044715 * v * v * v)))


def gather_rows_kernel(count, *refs):
    weights, out, rows = refs[:count], refs[-2], refs[-1]
    rows[...] = jnp.zeros_like(rows)
    for m, w in enumerate(weights):
        rows[6 * m : 6 * m + 6] = w[...].astype(F32)
    if len(refs) == count + 3:
        row = lax.broadcasted_iota(jnp.int32, (8, 128), 0)
        lane = lax.broadcasted_iota(jnp.int32, (8, 128), 1)
        unit = (row == lane).astype(F32)
        wide = jnp.concatenate([refs[count][...], jnp.zeros((120, 128), F32)], axis=0)
        rows[6 * count : 6 * count + 6, :128] = dot_t(unit, wide)[:6]
    out[...] = rows[...].astype(BF)


def packed_rows(weights, norms=()):
    count = len(weights)
    total = -(-(6 * count + (6 if norms else 0)) // 8) * 8
    more = [jnp.pad(jnp.stack(norms).astype(F32), ((0, 5), (0, 122)))] if norms else []
    return pl.pallas_call(
        functools.partial(gather_rows_kernel, count),
        out_shape=jax.ShapeDtypeStruct((total, 768), BF),
        scratch_shapes=[pltpu.VMEM((total, 768), F32)],
        compiler_params=PARAMS,
        cost_estimate=cost(2),
        name="packed_rows",
    )(*weights, *more)


def unpack_kernel(place_ref, packed_ref, *outs):
    for b in range(4):
        halves = [
            dot(place_ref[...], packed_ref[448 * b + 224 * n : 448 * b + 224 * n + 224])
            for n in range(2)
        ]
        for m, out in enumerate(outs):
            rows = jnp.concatenate([h[24 * m : 24 * m + 24] for h in halves], axis=0)
            out[48 * b : 48 * b + 48] = rows[:, : out.shape[1]].astype(BF)


def unpack(packed):
    q = jnp.arange(216, dtype=jnp.int32)
    source = (q % 24) // 6 * 56 + q // 24 * 6 + q % 6
    place = (source[:, None] == jnp.arange(224, dtype=jnp.int32)[None, :]).astype(BF)
    widths = [768] * 8 + [128]
    return pl.pallas_call(
        unpack_kernel,
        grid=(4,),
        in_specs=[
            pl.BlockSpec((216, 224), lambda b: (0, 0)),
            pl.BlockSpec((1792, 768), lambda b: (b, 0)),
        ],
        out_specs=[pl.BlockSpec((192, w), lambda b: (b, 0)) for w in widths],
        out_shape=[jax.ShapeDtypeStruct((768, w), BF) for w in widths],
        compiler_params=PARAMS,
        cost_estimate=cost(9),
        name="unpack",
    )(place, packed)


def weight_grads_kernel(
    place_ref, own_ref, other_ref, tokens_ref, dq_ref, dq_other_ref, dk_ref, dv_ref, out_own_ref, out_other_ref, *rest
):
    out_ref = rest[-1]
    n = pl.program_id(0)
    four = [
        dot(own_ref[:, :128], dq_ref[...]) + dot(other_ref[:, :128], dq_other_ref[...]),
        dot(tokens_ref[...], dk_ref[...]),
        dot(tokens_ref[...], dv_ref[...]),
        dot(own_ref[:, 128:], out_own_ref[...]) + dot(other_ref[:, 128:], out_other_ref[...]),
    ]
    four = [w.astype(BF) for w in four]
    columns = pl.ds(pl.multiple_of(n * 256, 256), 256)
    for b in range(8):
        rows = jnp.concatenate([w[48 * b : 48 * b + 48] for w in four], axis=0)
        out_ref[192 * b : 192 * b + 192, columns] = dot(place_ref[...], rows).astype(BF)
    if len(rest) == 2:

        @pl.when(n == 0)
        def _():
            out_ref[:, 768:] = rest[0][...]


def weight_grads(own, other, tokens, back, back_other, dk, dv, low, low_other, extra=None):
    p = jnp.arange(192, dtype=jnp.int32)
    source = (p % 24) // 6 * 48 + p // 24 * 6 + p % 6
    place = (source[:, None] == p[None, :]).astype(BF)
    width = 768 if extra is None else 896
    more = [] if extra is None else [extra.reshape(1536, 128)]
    whole = lambda a: pl.BlockSpec(a.shape, lambda n: (0, 0))
    first = pl.BlockSpec((128, 256), lambda n: (0, n))
    every = pl.BlockSpec((dk.shape[0], 256), lambda n: (0, n))
    return pl.pallas_call(
        weight_grads_kernel,
        grid=(3,),
        in_specs=[whole(place), whole(own), whole(other), whole(tokens), first, first, every, every, first, first]
        + [whole(a) for a in more],
        out_specs=pl.BlockSpec((1536, width), lambda n: (0, 0)),
        out_shape=jax.ShapeDtypeStruct((1536, width), BF),
        compiler_params=PARAMS,
        cost_estimate=cost(5),
        name="weight_grads",
    )(place, own, other, tokens, back, back_other, dk, dv, low, low_other, *more).reshape(64, 24, width)


def bias_kernel(line_ref, out_ref):
    for k in range(8):
        segment = line_ref[0, :, 128 * (7 - k) : 128 * (7 - k) + 256]
        wide = jnp.broadcast_to(segment, (128, 256))
        tile = pltpu.roll(wide, 129, 1, stride=1, stride_axis=0)
        out_ref[0, k] = tile[:, :128].astype(BF)


def bias_tiles(line):
    return pl.pallas_call(
        bias_kernel,
        grid=(HEADS,),
        in_specs=[pl.BlockSpec((1, 1, 1152), lambda h: (h, 0, 0))],
        out_specs=pl.BlockSpec((1, 8, 128, 128), lambda h: (h, 0, 0, 0)),
        out_shape=jax.ShapeDtypeStruct((HEADS, 8, 128, 128), BF),
        compiler_params=PARAMS,
        cost_estimate=cost(7.5),
        name="bias_tiles",
    )(line)


def half_lanes(shape, half):
    lane = lax.broadcasted_iota(jnp.int32, shape, 1)
    return (lane >= 64) if half else (lane < 64)


def block_offsets(place_ref):
    s, c, x = place_ref[0], place_ref[1], place_ref[2]
    return [
        s - (2 * lax.rem(x + n, 4) + (c if e == 0 else 1 - c)) for e in range(2) for n in range(4)
    ]


def add_bias(raw, bias_ref, half, away):
    i = lax.broadcasted_iota(jnp.int32, (128, 128), 0)
    j = lax.broadcasted_iota(jnp.int32, (128, 128), 1)
    parts = []
    for n, k in enumerate(away):
        tile = bias_ref[half, jnp.clip(k, 0, 7)].astype(F32)
        parts.append(
            jnp.where(i - j + 128 * k >= 0, raw[:, 128 * n : 128 * n + 128] + tile, MASKED)
        )
    return jnp.concatenate(parts, axis=1)


def forward_kernel(causal, pairs, place_ref, q_ref, k_ref, v_ref, *rest):
    bias_ref, out_ref = rest if causal else (None, rest[0])
    away = block_offsets(place_ref) if causal else None
    for pair in range(pairs):
        lanes = slice(128 * pair, 128 * pair + 128)
        keys, values, query = k_ref[:, lanes], v_ref[:, lanes], q_ref[:, lanes]
        mixed = []
        for half in range(2):
            low = half_lanes(query.shape, half)
            scores = dot_t(jnp.where(low, query, jnp.zeros_like(query)), keys)
            if causal:
                scores = add_bias(scores, bias_ref, 2 * pair + half, away)
            parts = jnp.exp(scores - jnp.max(scores, axis=-1, keepdims=True))
            share = 1.0 / jnp.sum(parts, axis=-1, keepdims=True)
            mixed.append(dot(parts.astype(BF), values) * share)
        out_ref[:, lanes] = jnp.where(half_lanes(mixed[0].shape, 0), mixed[0], mixed[1]).astype(BF)


def attend(place, query, keys, values, bias=None):
    causal = bias is not None
    rows, length = query.shape[0], keys.shape[0]
    pairs = 2 if causal else 6
    wide = 128 * pairs
    in_specs = [
        pl.BlockSpec(memory_space=pltpu.SMEM),
        pl.BlockSpec((rows, wide), lambda p: (0, p)),
        pl.BlockSpec((length, wide), lambda p: (0, p)),
        pl.BlockSpec((length, wide), lambda p: (0, p)),
    ]
    if causal:
        in_specs.append(pl.BlockSpec((2 * pairs, 8, 128, 128), lambda p: (p, 0, 0, 0)))
    return pl.pallas_call(
        functools.partial(forward_kernel, causal, pairs),
        grid=(PAIRS // pairs,),
        in_specs=in_specs,
        out_specs=pl.BlockSpec((rows, wide), lambda p: (0, p)),
        out_shape=jax.ShapeDtypeStruct((rows, 768), BF),
        compiler_params=PARAMS,
        cost_estimate=cost(7.5 if causal else 3),
        name="self_forward" if causal else "cross_forward",
    )(place, query, keys, values, *((bias,) if causal else ()))


def diagonal_sums(t):
    rows, width = t.shape
    while rows > 8:
        rows //= 2
        t = t[:rows] + pltpu.roll(t[rows:], width - rows, 1)
    row = lax.broadcasted_iota(jnp.int32, t.shape, 0)
    for step in (4, 2, 1):
        t = jnp.where((row & step) != 0, pltpu.roll(t, width - step, 1), t)
    return jnp.sum(t, axis=0, keepdims=True)


def backward_kernel(causal, pairs, place_ref, q_ref, k_ref, v_ref, g_ref, *rest):
    rows, length = q_ref.shape[0], k_ref.shape[0]
    if causal:
        bias_ref, out_ref, sums_ref, line_ref = rest
        away = block_offsets(place_ref)
        line_ref[:, :, length:] = jnp.zeros((2 * pairs, rows, 128), F32)
    else:
        (out_ref,) = rest
    for pair in range(pairs):
        lanes = slice(128 * pair, 128 * pair + 128)
        keys, values, query, grads = k_ref[:, lanes], v_ref[:, lanes], q_ref[:, lanes], g_ref[:, lanes]
        dq, dk, dv = [], 0.0, 0.0
        for half in range(2):
            low = half_lanes(query.shape, half)
            own_query = jnp.where(low, query, jnp.zeros_like(query))
            own_grads = jnp.where(low, grads, jnp.zeros_like(grads))
            scores = dot_t(own_query, keys)
            if causal:
                scores = add_bias(scores, bias_ref, 2 * pair + half, away)
            parts = jnp.exp(scores - jnp.max(scores, axis=-1, keepdims=True))
            shares = parts * (1.0 / jnp.sum(parts, axis=-1, keepdims=True))
            pushed = dot_t(own_grads, values)
            center = jnp.sum(shares * pushed, axis=-1, keepdims=True)
            ds = shares * (pushed - center)
            low_ds = ds.astype(BF)
            dq.append(dot(low_ds, keys))
            dk = dk + t_dot(low_ds, own_query)
            dv = dv + t_dot(shares.astype(BF), own_grads)
            if causal:
                for n, k in enumerate(away):
                    at = pl.multiple_of((place_ref[0] - k) * 128, 128)
                    line_ref[2 * pair + half, :, pl.ds(at, 128)] = ds[:, 128 * n : 128 * n + 128]
        out_ref[:rows, lanes] = jnp.where(half_lanes(dq[0].shape, 0), dq[0], dq[1]).astype(BF)
        out_ref[rows : rows + length, lanes] = dk.astype(BF)
        out_ref[rows + length :, lanes] = dv.astype(BF)
    if causal:
        for head in range(2 * pairs):
            sums_ref[head] = diagonal_sums(line_ref[head])


def attend_back(place, query, keys, values, grads, bias=None):
    causal = bias is not None
    rows, length = query.shape[0], keys.shape[0]
    pairs = 2 if causal else 6
    wide = 128 * pairs
    total = rows + 2 * length
    some = pl.BlockSpec((rows, wide), lambda p: (0, p))
    every = pl.BlockSpec((length, wide), lambda p: (0, p))
    in_specs = [pl.BlockSpec(memory_space=pltpu.SMEM), some, every, every, some]
    out_specs = [pl.BlockSpec((total, wide), lambda p: (0, p))]
    out_shape = [jax.ShapeDtypeStruct((total, 768), BF)]
    scratch = []
    if causal:
        in_specs.append(pl.BlockSpec((2 * pairs, 8, 128, 128), lambda p: (p, 0, 0, 0)))
        out_specs.append(pl.BlockSpec((2 * pairs, 1, length + 128), lambda p: (p, 0, 0)))
        out_shape.append(jax.ShapeDtypeStruct((HEADS, 1, length + 128), F32))
        scratch.append(pltpu.VMEM((2 * pairs, rows, length + 128), F32))
    return pl.pallas_call(
        functools.partial(backward_kernel, causal, pairs),
        grid=(PAIRS // pairs,),
        in_specs=in_specs,
        out_specs=out_specs,
        out_shape=out_shape,
        scratch_shapes=scratch,
        compiler_params=PARAMS,
        cost_estimate=cost(14.5 if causal else 2),
        name="self_backward" if causal else "cross_backward",
    )(place, query, keys, values, grads, *((bias,) if causal else ()))


def body(
    inputs,
    encoded,
    cotangent,
    buckets,
    bias_table,
    norm_self,
    norm_cross,
    norm_feed,
    self_query,
    self_key,
    self_value,
    self_out,
    cross_query,
    cross_key,
    cross_value,
    cross_out,
    feed_gate,
    feed_up,
    feed_down,
):
    core = lax.axis_index("c")
    place_x = lax.axis_index("x")
    place = jnp.stack([place_x * 2 + core, core, place_x]).astype(jnp.int32)

    packed = packed_rows(
        (
            self_query,
            self_key,
            self_value,
            self_out,
            cross_query,
            cross_key,
            cross_value,
            cross_out,
        ),
        (norm_self, norm_cross, norm_feed),
    )
    packed = lax.all_gather(packed, ALL, axis=0, tiled=True)

    def by_owner(w):
        return w.reshape(6, 16, 8, 16).transpose(2, 0, 1, 3).reshape(8, 6, 256)

    gate_up = jnp.concatenate([by_owner(feed_gate), by_owner(feed_up)], axis=2)
    gate_up_sent = exchange(gate_up, SEQ).reshape(48, 512)

    first = jnp.concatenate([inputs[0], encoded[0]], axis=0)
    first_own, first_other = around_x(first)
    first_own, first_other = first_own.reshape(4, 160, 768), first_other.reshape(4, 160, 768)
    cot = cotangent[0]

    ids = jnp.arange(32, dtype=jnp.int32)
    flipped = jnp.concatenate([buckets[::-1], jnp.full((128,), -1, jnp.int32)])
    hits = (flipped[None, :] == ids[:, None]).astype(BF)
    line = dot(bias_table.T, hits)
    tiles = bias_tiles(line.reshape(HEADS, 1, 1152))

    feed = jnp.concatenate(
        [gate_up_sent, feed_down[:, :512], jnp.pad(feed_down[:, 512:], ((0, 0), (0, 256)))], axis=0
    )
    feed = gathered(feed, "z").reshape(320, 512)
    feed = gathered(feed, "y").reshape(16, 80, 512)
    cot_own, cot_other = around_x(after(cot, first_own))
    states = jnp.concatenate([first_own[:, 128:], first_other[:, 128:]], axis=0).reshape(256, 768)

    f = jnp.arange(768, dtype=jnp.int32)
    n = jnp.arange(384, dtype=jnp.int32)
    pick = (f[None, :] == (n // 6 * 12 + 6 * core + n % 6)[:, None]).astype(BF)

    def picked(a):
        return dot_t(pick, a).astype(BF)

    low_states = picked(states)

    flipped = jnp.concatenate(
        [jnp.full((128,), -1, jnp.int32), flipped[:1024], jnp.full((1024,), -1, jnp.int32)]
    )
    start = 1151 - 128 * place[0]
    around = jnp.concatenate(
        [
            lax.dynamic_slice(flipped, (start,), (1024,)),
            lax.dynamic_slice(flipped, (start - 128,), (128,)),
        ]
    )
    table_hits = (around[:, None] == ids[None, :]).astype(F32)

    (
        packed, first_own, first_other, states, low_states, tiles, table_hits, pick, feed, cot_own, cot_other,
    ) = lax.optimization_barrier(
        (packed, first_own, first_other, states, low_states, tiles, table_hits, pick, feed, cot_own, cot_other)
    )

    w_q, w_k, w_v, w_o, c_q, c_k, c_v, c_o, gains = unpack(packed)
    gains = gains[:, :3].astype(F32).T
    gain_self, gain_cross, gain_feed = gains[0:1], gains[1:2], gains[2:3]

    x = inputs[0].astype(F32)
    x_all = jnp.concatenate([first_own[:, :128], first_other[:, :128]], axis=0)
    x_all = x_all.reshape(1024, 768).astype(F32)

    hat_all, _ = normed(x_all)
    low_all = (hat_all * gain_self).astype(BF)
    hat_one, r_one = normed(x)
    low_one = (hat_one * gain_self).astype(BF)
    query = dot(low_one, w_q).astype(BF)
    keys = dot(low_all, w_k).astype(BF)
    values = dot(low_all, w_v).astype(BF)
    mixed = attend(place, query, keys, values, tiles)
    gate_up = feed[:, :48].reshape(768, 512)
    down = jnp.concatenate([feed[:, 48:64], feed[:, 64:, :256]], axis=2).reshape(256, 768)
    after_self = x + dot(mixed, w_o)
    hat_two, r_two = normed(after_self)
    low_two = (hat_two * gain_cross).astype(BF)
    query_two = dot(low_two, c_q).astype(BF)
    keys_two = dot(states, c_k).astype(BF)
    values_two = dot(states, c_v).astype(BF)
    mixed_two = attend(place, query_two, keys_two, values_two)
    after_cross = after_self + dot(mixed_two, c_o)
    hat_three, r_three = normed(after_cross)
    low_three = (hat_three * gain_feed).astype(BF)

    left_self = jnp.concatenate([low_one, mixed], axis=0)
    left_cross = jnp.concatenate([low_two, mixed_two], axis=0)
    other_self, other_cross = other_core(left_self), other_core(left_cross)
    left_self, left_cross, other_self, other_cross = (
        picked(after(a, low_three)) for a in (left_self, left_cross, other_self, other_cross)
    )
    low_picked = picked(after(low_all, low_three))

    def feed_half(low, cot_half):
        both = dot(low, gate_up)
        gate, upper = both[:, :256], both[:, 256:]
        tanh = jnp.tanh(0.7978845608028654 * (gate + 0.044715 * gate * gate * gate))
        gelu_gate = 0.5 * gate * (1.0 + tanh)
        slope = 0.5 * (1.0 + tanh) + 0.5 * gate * (1.0 - tanh * tanh) * (
            0.7978845608028654 * (1.0 + 3.0 * 0.044715 * gate * gate)
        )
        hidden = (gelu_gate * upper).astype(BF)
        grad_hidden = dot_t(cot_half, down)
        low_gate = (grad_hidden * upper * slope).astype(BF)
        low_upper = (grad_hidden * gelu_gate).astype(BF)
        low_both = jnp.concatenate([low_gate, low_upper], axis=1)
        part_three = dot_t(low_both, gate_up).astype(BF)
        return hidden, low_both, part_three

    low_own, low_other = around_x(low_three)
    hidden_a, both_a, three_a = feed_half(low_own, cot_own)
    hidden_b, both_b, three_b = feed_half(low_other, cot_other)
    grad_low_three = back_around_x(core_sum(three_a, three_b))
    out_a = dot(hidden_a, down).astype(BF)
    out_b = dot(hidden_b, down).astype(BF)
    d_both = (t_dot(low_own, both_a) + t_dot(low_other, both_b)).astype(BF).reshape(16, 48, 512)
    d_down = (t_dot(hidden_a, cot_own) + t_dot(hidden_b, cot_other)).astype(BF).reshape(16, 16, 768)
    d_feed = jnp.concatenate(
        [d_both, d_down[:, :, :512], jnp.pad(d_down[:, :, 512:], ((0, 0), (0, 0), (0, 256)))], axis=1
    )
    part_out = core_sum(out_a, out_b)
    grad_low_three, part_out, left_self, left_cross, other_self, other_cross, low_picked = lax.optimization_barrier(
        (grad_low_three, part_out, left_self, left_cross, other_self, other_cross, low_picked)
    )
    output = (after_cross + back_around_x(part_out)).astype(BF)[None]
    d_feed = jnp.sum(exchange(d_feed, ROWS).astype(F32), axis=0)
    d_down = jnp.concatenate([d_feed[48:64], d_feed[64:80, :256]], axis=1)
    d_both = exchange(d_feed[:48].reshape(8, 6, 512), SEQ)

    def to_columns(part):
        return part.reshape(8, 6, 16, 16).transpose(1, 2, 0, 3).reshape(6, 2048)


    g_norm_feed = jnp.sum(grad_low_three * hat_three, axis=0)
    grad_two = cot.astype(F32) + norm_back(grad_low_three, hat_three, r_three, gain_feed)

    low_cross = grad_two.astype(BF)
    grad_mixed_two = dot_t(low_cross, c_o).astype(BF)
    (back_two,) = attend_back(place, query_two, keys_two, values_two, grad_mixed_two)
    back_two = after(back_two, d_feed)
    grad_low_two = dot_t(back_two[:128], c_q)
    g_norm_cross = jnp.sum(grad_low_two * hat_two, axis=0)
    grad_one = grad_two + norm_back(grad_low_two, hat_two, r_two, gain_cross)
    low_self = grad_one.astype(BF)

    def summed(a, b):
        half = a.shape[0] // 2
        b = jnp.concatenate([b[half:], b[:half]], axis=0)
        return (a.astype(F32) + b.astype(F32)).astype(BF)

    low_cross_other = other_core(low_cross)
    back_other = other_core(back_two)
    dk_two = summed(back_two[128:384], back_other[128:384])
    dv_two = summed(back_two[384:], back_other[384:])
    part_states = (dot_t(dk_two[:128], c_k) + dot_t(dv_two[:128], c_v)).astype(BF)

    grad_mixed = dot_t(low_self, w_o).astype(BF)
    low_self_other = other_core(low_self)
    back, sums = attend_back(place, query, keys, values, grad_mixed, tiles)
    back, output, dk_two, d_both = lax.optimization_barrier((back, output, dk_two, d_both))
    d_cross = weight_grads(
        left_cross, other_cross, low_states, back_two, back_other, dk_two, dv_two, low_cross, low_cross_other
    )
    d_cross = exchange(d_cross, CHIPS)
    back_other = other_core(back)
    dq = back[:128]
    dk = summed(back[128:1152], back_other[128:1152])
    dv = summed(back[1152:], back_other[1152:])
    part_one = dot_t(dk[:512], w_k) + dot_t(dv[:512], w_v)
    own_one = dot_t(dq, w_q)
    g_norm_self = jnp.sum(part_one * hat_all[:512], axis=0) + jnp.sum(own_one * hat_one, axis=0)

    table = lax.dot_general(
        table_hits, sums.reshape(HEADS, 1152), (((0,), (1,)), ((), ())), precision=lax.Precision.HIGHEST
    )
    scales = jnp.stack([g_norm_self, g_norm_cross, g_norm_feed])
    table, scales = table + other_core(table), scales + other_core(scales)
    scales = scales.reshape(3, 64, 12)
    scales = jnp.pad(scales.transpose(1, 0, 2), ((0, 0), (0, 0), (0, 116)))
    small = jnp.concatenate([scales, jnp.broadcast_to(table.reshape(1, 3, 128), (64, 3, 128))], axis=1)
    high = lax.reduce_precision(small, 8, 7)
    rest = (small - high).astype(BF)
    extra = jnp.concatenate([high.astype(BF), rest, jnp.zeros((64, 12, 128), BF)], axis=1)

    d_self = weight_grads(
        left_self, other_self, low_picked, back, back_other, dk, dv, low_self, low_self_other, extra
    )

    parts = jnp.concatenate(
        [part_one.astype(BF).reshape(4, 128, 768), part_states.reshape(4, 32, 768)], axis=1
    )
    arrived = back_around_x(parts.reshape(640, 768), d_self)
    grad_low_one = own_one + arrived[:128]
    grad_encoded = arrived[128:][None]
    grad_inputs = (grad_one + norm_back(grad_low_one, hat_one, r_one, gain_self))[None]
    d_self = jnp.sum(exchange(after(d_self, d_cross), CHIPS).astype(F32), axis=0)
    d_cross = jnp.sum(d_cross.astype(F32), axis=0)
    d_gate, d_up = to_columns(d_both[:, :, :256]), to_columns(d_both[:, :, 256:])

    small = d_self[:6, 768:] + d_self[6:12, 768:]
    table_grad = small[3:6].reshape(32, 12)
    scales = jnp.where(core == 0, small[:3, :6], small[:3, 6:12])
    d_self = d_self[:, :768]

    return (
        output,
        grad_inputs,
        grad_encoded,
        table_grad,
        scales[0],
        scales[1],
        scales[2],
        d_self[0:6],
        d_self[6:12],
        d_self[12:18],
        d_self[18:24],
        d_cross[0:6],
        d_cross[6:12],
        d_cross[12:18],
        d_cross[18:24],
        d_gate,
        d_up,
        d_down,
    )


def solution(mesh):
    finer = Mesh(mesh.devices.reshape(4, 4, 4, 2), ALL)
    tokens = P(ROWS, SEQ, None)
    scale, weight = P(ALL), P(ALL, None)
    return jax.shard_map(
        body,
        mesh=finer,
        in_specs=(tokens, tokens, tokens, P(), P(), *([scale] * 3), *([weight] * 11)),
        out_specs=(tokens, tokens, tokens, P(), *([scale] * 3), *([weight] * 11)),
        check_vma=False,
    )
```

```python
import functools

import jax
import jax.numpy as jnp
from jax import lax
from jax.experimental import pallas as pl
from jax.experimental.pallas import tpu as pltpu
from jax.sharding import Mesh
from jax.sharding import PartitionSpec as P

HEADS = 12
PAIRS = HEADS // 2
EPS = 1e-06
MASKED = -1e30
BF = jnp.bfloat16
F32 = jnp.float32
ALL = ("y", "z", "x", "c")
CHIPS = ("y", "z", "x")
ROWS = ("y", "z")
SEQ = ("x", "c")
SWAP = [(0, 1), (1, 0)]
PARAMS = pltpu.CompilerParams(vmem_limit_bytes=56 * 1024 * 1024)


def other_core(a):
    return lax.ppermute(a, "c", SWAP)


def exchange(a, axes):
    return lax.all_to_all(a, axes, 0, 0, tiled=True)


def copies(a, axes, count):
    return exchange(jnp.broadcast_to(a[None], (count, *a.shape)), axes)


def shifted(a, by):
    return lax.ppermute(a, "x", [((i + by) % 4, i) for i in range(4)])


def around_x(a):
    own = jnp.concatenate([a, *(shifted(a, by) for by in (1, 2, 3))], axis=0)
    return own, other_core(own)


def gathered(a, axis):
    place = lax.axis_index(axis)
    whole = jnp.zeros((4, *a.shape), a.dtype)
    for by in range(4):
        part = a
        if by:
            part = lax.ppermute(a, axis, [((i + by) % 4, i) for i in range(4)])
        whole = lax.dynamic_update_index_in_dim(whole, part, lax.rem(place + by, 4), 0)
    return whole


def back_around_x(parts, *earlier):
    rows = parts.shape[0] // 4
    own, *others = [parts[rows * n : rows * n + rows] for n in range(4)]
    others = [shifted(a, -by) for by, a in enumerate(others, 1)]
    if earlier:
        others = lax.optimization_barrier((*others, *earlier))[:3]
    return own.astype(F32) + sum(a.astype(F32) for a in others)


def core_sum(own, other):
    return (own.astype(F32) + other_core(other).astype(F32)).astype(BF)


def after(a, *earlier):
    return lax.optimization_barrier((a, *earlier))[0]


def cost(us):
    return pl.CostEstimate(flops=int(us * 1.0e9), bytes_accessed=int(us * 1.0e6), transcendentals=0)


def dot(a, b):
    return jnp.dot(a, b, preferred_element_type=F32)


def dot_t(a, b):
    return lax.dot_general(a, b, (((1,), (1,)), ((), ())), preferred_element_type=F32)


def t_dot(a, b):
    return lax.dot_general(a, b, (((0,), (0,)), ((), ())), preferred_element_type=F32)


def normed(v):
    r = lax.rsqrt(jnp.mean(v * v, axis=-1, keepdims=True) + EPS)
    return v * r, r


def norm_back(g, hat, r, gain):
    scaled = g * gain
    return r * (scaled - hat * jnp.mean(scaled * hat, axis=-1, keepdims=True))


def gelu(v):
    return 0.5 * v * (1.0 + jnp.tanh(0.7978845608028654 * (v + 0.044715 * v * v * v)))


def gather_rows_kernel(count, *refs):
    weights, out, rows = refs[:count], refs[-2], refs[-1]
    rows[...] = jnp.zeros_like(rows)
    for m, w in enumerate(weights):
        rows[6 * m : 6 * m + 6] = w[...].astype(F32)
    if len(refs) == count + 3:
        row = lax.broadcasted_iota(jnp.int32, (8, 128), 0)
        lane = lax.broadcasted_iota(jnp.int32, (8, 128), 1)
        unit = (row == lane).astype(F32)
        wide = jnp.concatenate([refs[count][...], jnp.zeros((120, 128), F32)], axis=0)
        rows[6 * count : 6 * count + 6, :128] = dot_t(unit, wide)[:6]
    out[...] = rows[...].astype(BF)


def packed_rows(weights, norms=()):
    count = len(weights)
    total = -(-(6 * count + (6 if norms else 0)) // 8) * 8
    more = [jnp.pad(jnp.stack(norms).astype(F32), ((0, 5), (0, 122)))] if norms else []
    return pl.pallas_call(
        functools.partial(gather_rows_kernel, count),
        out_shape=jax.ShapeDtypeStruct((total, 768), BF),
        scratch_shapes=[pltpu.VMEM((total, 768), F32)],
        compiler_params=PARAMS,
        cost_estimate=cost(2),
        name="packed_rows",
    )(*weights, *more)


def unpack_kernel(place_ref, packed_ref, *outs):
    for b in range(4):
        halves = [
            dot(place_ref[...], packed_ref[448 * b + 224 * n : 448 * b + 224 * n + 224])
            for n in range(2)
        ]
        for m, out in enumerate(outs):
            rows = jnp.concatenate([h[24 * m : 24 * m + 24] for h in halves], axis=0)
            out[48 * b : 48 * b + 48] = rows[:, : out.shape[1]].astype(BF)


def unpack(packed):
    q = jnp.arange(216, dtype=jnp.int32)
    source = (q % 24) // 6 * 56 + q // 24 * 6 + q % 6
    place = (source[:, None] == jnp.arange(224, dtype=jnp.int32)[None, :]).astype(BF)
    widths = [768] * 8 + [128]
    return pl.pallas_call(
        unpack_kernel,
        grid=(4,),
        in_specs=[
            pl.BlockSpec((216, 224), lambda b: (0, 0)),
            pl.BlockSpec((1792, 768), lambda b: (b, 0)),
        ],
        out_specs=[pl.BlockSpec((192, w), lambda b: (b, 0)) for w in widths],
        out_shape=[jax.ShapeDtypeStruct((768, w), BF) for w in widths],
        compiler_params=PARAMS,
        cost_estimate=cost(9),
        name="unpack",
    )(place, packed)


def weight_grads_kernel(
    place_ref, own_ref, other_ref, tokens_ref, dq_ref, dq_other_ref, dk_ref, dv_ref, out_own_ref, out_other_ref, *rest
):
    out_ref = rest[-1]
    n = pl.program_id(0)
    four = [
        dot(own_ref[:, :128], dq_ref[...]) + dot(other_ref[:, :128], dq_other_ref[...]),
        dot(tokens_ref[...], dk_ref[...]),
        dot(tokens_ref[...], dv_ref[...]),
        dot(own_ref[:, 128:], out_own_ref[...]) + dot(other_ref[:, 128:], out_other_ref[...]),
    ]
    four = [w.astype(BF) for w in four]
    columns = pl.ds(pl.multiple_of(n * 256, 256), 256)
    for b in range(8):
        rows = jnp.concatenate([w[48 * b : 48 * b + 48] for w in four], axis=0)
        out_ref[192 * b : 192 * b + 192, columns] = dot(place_ref[...], rows).astype(BF)
    if len(rest) == 2:

        @pl.when(n == 0)
        def _():
            out_ref[:, 768:] = rest[0][...]


def weight_grads(own, other, tokens, back, back_other, dk, dv, low, low_other, extra=None):
    p = jnp.arange(192, dtype=jnp.int32)
    source = (p % 24) // 6 * 48 + p // 24 * 6 + p % 6
    place = (source[:, None] == p[None, :]).astype(BF)
    width = 768 if extra is None else 896
    more = [] if extra is None else [extra.reshape(1536, 128)]
    whole = lambda a: pl.BlockSpec(a.shape, lambda n: (0, 0))
    first = pl.BlockSpec((128, 256), lambda n: (0, n))
    every = pl.BlockSpec((dk.shape[0], 256), lambda n: (0, n))
    return pl.pallas_call(
        weight_grads_kernel,
        grid=(3,),
        in_specs=[whole(place), whole(own), whole(other), whole(tokens), first, first, every, every, first, first]
        + [whole(a) for a in more],
        out_specs=pl.BlockSpec((1536, width), lambda n: (0, 0)),
        out_shape=jax.ShapeDtypeStruct((1536, width), BF),
        compiler_params=PARAMS,
        cost_estimate=cost(5),
        name="weight_grads",
    )(place, own, other, tokens, back, back_other, dk, dv, low, low_other, *more).reshape(64, 24, width)


def bias_kernel(line_ref, out_ref):
    for k in range(8):
        segment = line_ref[0, :, 128 * (7 - k) : 128 * (7 - k) + 256]
        wide = jnp.broadcast_to(segment, (128, 256))
        tile = pltpu.roll(wide, 129, 1, stride=1, stride_axis=0)
        out_ref[0, k] = tile[:, :128].astype(BF)


def bias_tiles(line):
    return pl.pallas_call(
        bias_kernel,
        grid=(HEADS,),
        in_specs=[pl.BlockSpec((1, 1, 1152), lambda h: (h, 0, 0))],
        out_specs=pl.BlockSpec((1, 8, 128, 128), lambda h: (h, 0, 0, 0)),
        out_shape=jax.ShapeDtypeStruct((HEADS, 8, 128, 128), BF),
        compiler_params=PARAMS,
        cost_estimate=cost(7.5),
        name="bias_tiles",
    )(line)


def half_lanes(shape, half):
    lane = lax.broadcasted_iota(jnp.int32, shape, 1)
    return (lane >= 64) if half else (lane < 64)


def block_offsets(place_ref):
    s, c, x = place_ref[0], place_ref[1], place_ref[2]
    return [
        s - (2 * lax.rem(x + n, 4) + (c if e == 0 else 1 - c)) for e in range(2) for n in range(4)
    ]


def add_bias(raw, bias_ref, half, away):
    i = lax.broadcasted_iota(jnp.int32, (128, 128), 0)
    j = lax.broadcasted_iota(jnp.int32, (128, 128), 1)
    parts = []
    for n, k in enumerate(away):
        tile = bias_ref[half, jnp.clip(k, 0, 7)].astype(F32)
        parts.append(
            jnp.where(i - j + 128 * k >= 0, raw[:, 128 * n : 128 * n + 128] + tile, MASKED)
        )
    return jnp.concatenate(parts, axis=1)


def forward_kernel(causal, pairs, place_ref, q_ref, k_ref, v_ref, *rest):
    bias_ref, out_ref = rest if causal else (None, rest[0])
    away = block_offsets(place_ref) if causal else None
    for pair in range(pairs):
        lanes = slice(128 * pair, 128 * pair + 128)
        keys, values, query = k_ref[:, lanes], v_ref[:, lanes], q_ref[:, lanes]
        mixed = []
        for half in range(2):
            low = half_lanes(query.shape, half)
            scores = dot_t(jnp.where(low, query, jnp.zeros_like(query)), keys)
            if causal:
                scores = add_bias(scores, bias_ref, 2 * pair + half, away)
            parts = jnp.exp(scores - jnp.max(scores, axis=-1, keepdims=True))
            share = 1.0 / jnp.sum(parts, axis=-1, keepdims=True)
            mixed.append(dot(parts.astype(BF), values) * share)
        out_ref[:, lanes] = jnp.where(half_lanes(mixed[0].shape, 0), mixed[0], mixed[1]).astype(BF)


def attend(place, query, keys, values, bias=None):
    causal = bias is not None
    rows, length = query.shape[0], keys.shape[0]
    pairs = 2 if causal else 6
    wide = 128 * pairs
    in_specs = [
        pl.BlockSpec(memory_space=pltpu.SMEM),
        pl.BlockSpec((rows, wide), lambda p: (0, p)),
        pl.BlockSpec((length, wide), lambda p: (0, p)),
        pl.BlockSpec((length, wide), lambda p: (0, p)),
    ]
    if causal:
        in_specs.append(pl.BlockSpec((2 * pairs, 8, 128, 128), lambda p: (p, 0, 0, 0)))
    return pl.pallas_call(
        functools.partial(forward_kernel, causal, pairs),
        grid=(PAIRS // pairs,),
        in_specs=in_specs,
        out_specs=pl.BlockSpec((rows, wide), lambda p: (0, p)),
        out_shape=jax.ShapeDtypeStruct((rows, 768), BF),
        compiler_params=PARAMS,
        cost_estimate=cost(7.5 if causal else 3),
        name="self_forward" if causal else "cross_forward",
    )(place, query, keys, values, *((bias,) if causal else ()))


def diagonal_sums(t):
    rows, width = t.shape
    while rows > 8:
        rows //= 2
        t = t[:rows] + pltpu.roll(t[rows:], width - rows, 1)
    row = lax.broadcasted_iota(jnp.int32, t.shape, 0)
    for step in (4, 2, 1):
        t = jnp.where((row & step) != 0, pltpu.roll(t, width - step, 1), t)
    return jnp.sum(t, axis=0, keepdims=True)


def backward_kernel(causal, pairs, place_ref, q_ref, k_ref, v_ref, g_ref, *rest):
    rows, length = q_ref.shape[0], k_ref.shape[0]
    if causal:
        bias_ref, out_ref, sums_ref, line_ref = rest
        away = block_offsets(place_ref)
        line_ref[:, :, length:] = jnp.zeros((2 * pairs, rows, 128), F32)
    else:
        (out_ref,) = rest
    for pair in range(pairs):
        lanes = slice(128 * pair, 128 * pair + 128)
        keys, values, query, grads = k_ref[:, lanes], v_ref[:, lanes], q_ref[:, lanes], g_ref[:, lanes]
        dq, dk, dv = [], 0.0, 0.0
        for half in range(2):
            low = half_lanes(query.shape, half)
            own_query = jnp.where(low, query, jnp.zeros_like(query))
            own_grads = jnp.where(low, grads, jnp.zeros_like(grads))
            scores = dot_t(own_query, keys)
            if causal:
                scores = add_bias(scores, bias_ref, 2 * pair + half, away)
            parts = jnp.exp(scores - jnp.max(scores, axis=-1, keepdims=True))
            shares = parts * (1.0 / jnp.sum(parts, axis=-1, keepdims=True))
            pushed = dot_t(own_grads, values)
            center = jnp.sum(shares * pushed, axis=-1, keepdims=True)
            ds = shares * (pushed - center)
            low_ds = ds.astype(BF)
            dq.append(dot(low_ds, keys))
            dk = dk + t_dot(low_ds, own_query)
            dv = dv + t_dot(shares.astype(BF), own_grads)
            if causal:
                for n, k in enumerate(away):
                    at = pl.multiple_of((place_ref[0] - k) * 128, 128)
                    line_ref[2 * pair + half, :, pl.ds(at, 128)] = ds[:, 128 * n : 128 * n + 128]
        out_ref[:rows, lanes] = jnp.where(half_lanes(dq[0].shape, 0), dq[0], dq[1]).astype(BF)
        out_ref[rows : rows + length, lanes] = dk.astype(BF)
        out_ref[rows + length :, lanes] = dv.astype(BF)
    if causal:
        for head in range(2 * pairs):
            sums_ref[head] = diagonal_sums(line_ref[head])


def attend_back(place, query, keys, values, grads, bias=None):
    causal = bias is not None
    rows, length = query.shape[0], keys.shape[0]
    pairs = 2 if causal else 6
    wide = 128 * pairs
    total = rows + 2 * length
    some = pl.BlockSpec((rows, wide), lambda p: (0, p))
    every = pl.BlockSpec((length, wide), lambda p: (0, p))
    in_specs = [pl.BlockSpec(memory_space=pltpu.SMEM), some, every, every, some]
    out_specs = [pl.BlockSpec((total, wide), lambda p: (0, p))]
    out_shape = [jax.ShapeDtypeStruct((total, 768), BF)]
    scratch = []
    if causal:
        in_specs.append(pl.BlockSpec((2 * pairs, 8, 128, 128), lambda p: (p, 0, 0, 0)))
        out_specs.append(pl.BlockSpec((2 * pairs, 1, length + 128), lambda p: (p, 0, 0)))
        out_shape.append(jax.ShapeDtypeStruct((HEADS, 1, length + 128), F32))
        scratch.append(pltpu.VMEM((2 * pairs, rows, length + 128), F32))
    return pl.pallas_call(
        functools.partial(backward_kernel, causal, pairs),
        grid=(PAIRS // pairs,),
        in_specs=in_specs,
        out_specs=out_specs,
        out_shape=out_shape,
        scratch_shapes=scratch,
        compiler_params=PARAMS,
        cost_estimate=cost(14.5 if causal else 2),
        name="self_backward" if causal else "cross_backward",
    )(place, query, keys, values, grads, *((bias,) if causal else ()))


def body(
    inputs,
    encoded,
    cotangent,
    buckets,
    bias_table,
    norm_self,
    norm_cross,
    norm_feed,
    self_query,
    self_key,
    self_value,
    self_out,
    cross_query,
    cross_key,
    cross_value,
    cross_out,
    feed_gate,
    feed_up,
    feed_down,
):
    core = lax.axis_index("c")
    place_x = lax.axis_index("x")
    place = jnp.stack([place_x * 2 + core, core, place_x]).astype(jnp.int32)

    packed = packed_rows(
        (
            self_query,
            self_key,
            self_value,
            self_out,
            cross_query,
            cross_key,
            cross_value,
            cross_out,
        ),
        (norm_self, norm_cross, norm_feed),
    )
    packed = lax.all_gather(packed, ALL, axis=0, tiled=True)

    def by_owner(w):
        return w.reshape(6, 16, 8, 16).transpose(2, 0, 1, 3).reshape(8, 6, 256)

    gate_up = jnp.concatenate([by_owner(feed_gate), by_owner(feed_up)], axis=2)
    gate_up_sent = exchange(gate_up, SEQ).reshape(48, 512)

    first = jnp.concatenate([inputs[0], encoded[0]], axis=0)
    first_own, first_other = around_x(first)
    first_own, first_other = first_own.reshape(4, 160, 768), first_other.reshape(4, 160, 768)
    cot = cotangent[0]

    ids = jnp.arange(32, dtype=jnp.int32)
    flipped = jnp.concatenate([buckets[::-1], jnp.full((128,), -1, jnp.int32)])
    hits = (flipped[None, :] == ids[:, None]).astype(BF)
    line = dot(bias_table.T, hits)
    tiles = bias_tiles(line.reshape(HEADS, 1, 1152))

    feed = jnp.concatenate(
        [gate_up_sent, feed_down[:, :512], jnp.pad(feed_down[:, 512:], ((0, 0), (0, 256)))], axis=0
    )
    feed = gathered(feed, "z").reshape(320, 512)
    feed = gathered(feed, "y").reshape(16, 80, 512)
    cot_own, cot_other = around_x(after(cot, first_own))
    states = jnp.concatenate([first_own[:, 128:], first_other[:, 128:]], axis=0).reshape(256, 768)

    f = jnp.arange(768, dtype=jnp.int32)
    n = jnp.arange(384, dtype=jnp.int32)
    pick = (f[None, :] == (n // 6 * 12 + 6 * core + n % 6)[:, None]).astype(BF)

    def picked(a):
        return dot_t(pick, a).astype(BF)

    low_states = picked(states)

    flipped = jnp.concatenate(
        [jnp.full((128,), -1, jnp.int32), flipped[:1024], jnp.full((1024,), -1, jnp.int32)]
    )
    start = 1151 - 128 * place[0]
    around = jnp.concatenate(
        [
            lax.dynamic_slice(flipped, (start,), (1024,)),
            lax.dynamic_slice(flipped, (start - 128,), (128,)),
        ]
    )
    table_hits = (around[:, None] == ids[None, :]).astype(F32)

    (
        packed, first_own, first_other, states, low_states, tiles, table_hits, pick, feed, cot_own, cot_other,
    ) = lax.optimization_barrier(
        (packed, first_own, first_other, states, low_states, tiles, table_hits, pick, feed, cot_own, cot_other)
    )

    w_q, w_k, w_v, w_o, c_q, c_k, c_v, c_o, gains = unpack(packed)
    gains = gains[:, :3].astype(F32).T
    gain_self, gain_cross, gain_feed = gains[0:1], gains[1:2], gains[2:3]

    x = inputs[0].astype(F32)
    x_all = jnp.concatenate([first_own[:, :128], first_other[:, :128]], axis=0)
    x_all = x_all.reshape(1024, 768).astype(F32)

    hat_all, _ = normed(x_all)
    low_all = (hat_all * gain_self).astype(BF)
    hat_one, r_one = normed(x)
    low_one = (hat_one * gain_self).astype(BF)
    query = dot(low_one, w_q).astype(BF)
    keys = dot(low_all, w_k).astype(BF)
    values = dot(low_all, w_v).astype(BF)
    mixed = attend(place, query, keys, values, tiles)
    gate_up = feed[:, :48].reshape(768, 512)
    down = jnp.concatenate([feed[:, 48:64], feed[:, 64:, :256]], axis=2).reshape(256, 768)
    after_self = x + dot(mixed, w_o)
    hat_two, r_two = normed(after_self)
    low_two = (hat_two * gain_cross).astype(BF)
    query_two = dot(low_two, c_q).astype(BF)
    keys_two = dot(states, c_k).astype(BF)
    values_two = dot(states, c_v).astype(BF)
    mixed_two = attend(place, query_two, keys_two, values_two)
    after_cross = after_self + dot(mixed_two, c_o)
    hat_three, r_three = normed(after_cross)
    low_three = (hat_three * gain_feed).astype(BF)

    left_self = jnp.concatenate([low_one, mixed], axis=0)
    left_cross = jnp.concatenate([low_two, mixed_two], axis=0)
    other_self, other_cross = other_core(left_self), other_core(left_cross)
    left_self, left_cross, other_self, other_cross = (
        picked(after(a, low_three)) for a in (left_self, left_cross, other_self, other_cross)
    )
    low_picked = picked(after(low_all, low_three))

    def feed_half(low, cot_half):
        both = dot(low, gate_up)
        gate, upper = both[:, :256], both[:, 256:]
        tanh = jnp.tanh(0.7978845608028654 * (gate + 0.044715 * gate * gate * gate))
        gelu_gate = 0.5 * gate * (1.0 + tanh)
        slope = 0.5 * (1.0 + tanh) + 0.5 * gate * (1.0 - tanh * tanh) * (
            0.7978845608028654 * (1.0 + 3.0 * 0.044715 * gate * gate)
        )
        hidden = (gelu_gate * upper).astype(BF)
        grad_hidden = dot_t(cot_half, down)
        low_gate = (grad_hidden * upper * slope).astype(BF)
        low_upper = (grad_hidden * gelu_gate).astype(BF)
        low_both = jnp.concatenate([low_gate, low_upper], axis=1)
        part_three = dot_t(low_both, gate_up).astype(BF)
        return hidden, low_both, part_three

    low_own, low_other = around_x(low_three)
    hidden_a, both_a, three_a = feed_half(low_own, cot_own)
    hidden_b, both_b, three_b = feed_half(low_other, cot_other)
    grad_low_three = back_around_x(core_sum(three_a, three_b))
    out_a = dot(hidden_a, down).astype(BF)
    out_b = dot(hidden_b, down).astype(BF)
    d_both = (t_dot(low_own, both_a) + t_dot(low_other, both_b)).astype(BF).reshape(16, 48, 512)
    d_down = (t_dot(hidden_a, cot_own) + t_dot(hidden_b, cot_other)).astype(BF).reshape(16, 16, 768)
    d_feed = jnp.concatenate(
        [d_both, d_down[:, :, :512], jnp.pad(d_down[:, :, 512:], ((0, 0), (0, 0), (0, 256)))], axis=1
    )
    part_out = core_sum(out_a, out_b)
    grad_low_three, part_out, left_self, left_cross, other_self, other_cross, low_picked = lax.optimization_barrier(
        (grad_low_three, part_out, left_self, left_cross, other_self, other_cross, low_picked)
    )
    output = (after_cross + back_around_x(part_out)).astype(BF)[None]
    d_feed = jnp.sum(exchange(d_feed, ROWS).astype(F32), axis=0)
    d_down = jnp.concatenate([d_feed[48:64], d_feed[64:80, :256]], axis=1)
    d_both = exchange(d_feed[:48].reshape(8, 6, 512), SEQ)

    def to_columns(part):
        return part.reshape(8, 6, 16, 16).transpose(1, 2, 0, 3).reshape(6, 2048)


    g_norm_feed = jnp.sum(grad_low_three * hat_three, axis=0)
    grad_two = cot.astype(F32) + norm_back(grad_low_three, hat_three, r_three, gain_feed)

    low_cross = grad_two.astype(BF)
    grad_mixed_two = dot_t(low_cross, c_o).astype(BF)
    (back_two,) = attend_back(place, query_two, keys_two, values_two, grad_mixed_two)
    back_two = after(back_two, d_feed)
    grad_low_two = dot_t(back_two[:128], c_q)
    g_norm_cross = jnp.sum(grad_low_two * hat_two, axis=0)
    grad_one = grad_two + norm_back(grad_low_two, hat_two, r_two, gain_cross)
    low_self = grad_one.astype(BF)

    def summed(a, b):
        half = a.shape[0] // 2
        b = jnp.concatenate([b[half:], b[:half]], axis=0)
        return (a.astype(F32) + b.astype(F32)).astype(BF)

    low_cross_other = other_core(low_cross)
    back_other = other_core(back_two)
    dk_two = summed(back_two[128:384], back_other[128:384])
    dv_two = summed(back_two[384:], back_other[384:])
    part_states = (dot_t(dk_two[:128], c_k) + dot_t(dv_two[:128], c_v)).astype(BF)

    grad_mixed = dot_t(low_self, w_o).astype(BF)
    low_self_other = other_core(low_self)
    back, sums = attend_back(place, query, keys, values, grad_mixed, tiles)
    back, output, dk_two, d_both, low_cross_other, low_self_other = lax.optimization_barrier(
        (back, output, dk_two, d_both, low_cross_other, low_self_other)
    )
    d_cross = weight_grads(
        left_cross, other_cross, low_states, back_two, back_other, dk_two, dv_two, low_cross, low_cross_other
    )
    d_cross = exchange(d_cross, CHIPS)
    back_other = other_core(back)
    dq = back[:128]
    dk = summed(back[128:1152], back_other[128:1152])
    dv = summed(back[1152:], back_other[1152:])
    part_one = dot_t(dk[:512], w_k) + dot_t(dv[:512], w_v)
    own_one = dot_t(dq, w_q)
    g_norm_self = jnp.sum(part_one * hat_all[:512], axis=0) + jnp.sum(own_one * hat_one, axis=0)

    table = lax.dot_general(
        table_hits, sums.reshape(HEADS, 1152), (((0,), (1,)), ((), ())), precision=lax.Precision.HIGHEST
    )
    scales = jnp.stack([g_norm_self, g_norm_cross, g_norm_feed])
    table, scales = table + other_core(table), scales + other_core(scales)
    scales = scales.reshape(3, 64, 12)
    scales = jnp.pad(scales.transpose(1, 0, 2), ((0, 0), (0, 0), (0, 116)))
    small = jnp.concatenate([scales, jnp.broadcast_to(table.reshape(1, 3, 128), (64, 3, 128))], axis=1)
    high = lax.reduce_precision(small, 8, 7)
    rest = (small - high).astype(BF)
    extra = jnp.concatenate([high.astype(BF), rest, jnp.zeros((64, 12, 128), BF)], axis=1)

    d_self = weight_grads(
        left_self, other_self, low_picked, back, back_other, dk, dv, low_self, low_self_other, extra
    )

    parts = jnp.concatenate(
        [part_one.astype(BF).reshape(4, 128, 768), part_states.reshape(4, 32, 768)], axis=1
    )
    arrived = back_around_x(parts.reshape(640, 768), d_self)
    grad_low_one = own_one + arrived[:128]
    grad_encoded = arrived[128:][None]
    grad_inputs = (grad_one + norm_back(grad_low_one, hat_one, r_one, gain_self))[None]
    d_self = jnp.sum(exchange(after(d_self, d_cross), CHIPS).astype(F32), axis=0)
    d_cross = jnp.sum(d_cross.astype(F32), axis=0)
    d_gate, d_up = to_columns(d_both[:, :, :256]), to_columns(d_both[:, :, 256:])

    small = d_self[:6, 768:] + d_self[6:12, 768:]
    table_grad = small[3:6].reshape(32, 12)
    scales = jnp.where(core == 0, small[:3, :6], small[:3, 6:12])
    d_self = d_self[:, :768]

    return (
        output,
        grad_inputs,
        grad_encoded,
        table_grad,
        scales[0],
        scales[1],
        scales[2],
        d_self[0:6],
        d_self[6:12],
        d_self[12:18],
        d_self[18:24],
        d_cross[0:6],
        d_cross[6:12],
        d_cross[12:18],
        d_cross[18:24],
        d_gate,
        d_up,
        d_down,
    )


def solution(mesh):
    finer = Mesh(mesh.devices.reshape(4, 4, 4, 2), ALL)
    tokens = P(ROWS, SEQ, None)
    scale, weight = P(ALL), P(ALL, None)
    return jax.shard_map(
        body,
        mesh=finer,
        in_specs=(tokens, tokens, tokens, P(), P(), *([scale] * 3), *([weight] * 11)),
        out_specs=(tokens, tokens, tokens, P(), *([scale] * 3), *([weight] * 11)),
        check_vma=False,
    )
```
